128 devices in a mesh: dx: 8 (over z, core), dy: 16 (over y, x).
Axes of the slice: x: 4, y: 4, z: 4, core: 2. Of those that a mesh axis runs over, the one named last changes fastest.
Arguments:
- orbitals: bfloat16 [128, 64, 4096], P(('dx', 'dy')), may hold values from -6 to 6
- offsets: int32 [128, 3], replicated, may hold values from 0 to 31
- pair_list: int32 [1024, 2], P(('dx', 'dy')), may hold values from 0 to 127, as said below
- pair_mask: int32 [1024], P(('dx', 'dy')), may hold values from 0 to 1, as said below
Outputs:
- exchange: float32 [128, 64, 4096], P(('dx', 'dy'))
The draws below stay inside these ranges and needn't reach their ends.
Inputs may be any that keep to these rules, and one draw needn't show every extreme that they name: `pair_list`: in each spatial domain's block of 8 slots (domain index dx * 16 + dy owns orbitals 1 * that index onward), the first orbital belongs to that domain and the second to it or to one of the eight domains whose x and y domain indices differ by at most one, wrapping around. `pair_mask`: every domain uses at least one slot; in every draw some domain uses all 8.
All inputs are finite; a program needn't handle non-finite values.
Results may differ from the reference program's by a relative error of at most 0.0003.
Values may be sent and summed in bfloat16 or wider, within the bound.
No kernel may reach another device: no remote copies, remote signals or barrier semaphores. Data moves between devices by JAX's collectives and lax.ppermute only.
A program may use at most 64 MiB of HBM per device.

```python
import math
import jax
import jax.numpy as jnp
from jax import lax

BOX = 64
ORB_DEV = 1
PAIR_DEV = 8
DOM_X = 8
DOM_Y = 16
ORBS = 128


def draw_orbitals(key, part):
    key = jax.random.fold_in(key, 5)
    keys = jax.random.split(key, 4)
    waves = 4
    amplitude = 0.64
    lowest = BOX * 5 // 32
    highest = BOX * 15 // 32 + 1
    magnitude = jax.random.randint(keys[0], (waves, ORBS, 3), lowest, highest)
    signs = 2 * jax.random.randint(keys[1], (waves, ORBS, 3), 0, 2) - 1
    modes = (magnitude * signs).astype(jnp.int32)
    phases = jax.random.uniform(keys[2], (waves, ORBS), jnp.float32, -math.pi, math.pi)
    cell_x = jnp.arange(BOX, dtype=jnp.int32)
    flat_index = jnp.arange(BOX * BOX, dtype=jnp.int32)
    cell_y = flat_index // BOX
    cell_z = flat_index % BOX
    noise = 0.4 * jax.random.normal(keys[3], (ORBS, BOX, BOX * BOX), jnp.float32)
    factor = jnp.ones((ORBS,), jnp.float32)
    total = noise
    for which in range(waves):
        chosen = modes[which]
        turns = chosen[:, 0, None, None] * cell_x[None, :, None] + chosen[:, 1, None, None] * cell_y[None, None, :] + chosen[:, 2, None, None] * cell_z[None, None, :]
        turns = turns % BOX
        angle = 2.0 * math.pi / BOX * turns.astype(jnp.float32) + phases[which][:, None, None]
        total = total + amplitude * factor[:, None, None] * jnp.cos(angle)
    return jnp.clip(total, -6.0, 6.0).astype(jnp.bfloat16)


def draw_pair_list(key, part):
    key = jax.random.fold_in(key, 11)
    keys = jax.random.split(key, 4)
    domains = DOM_X * DOM_Y
    index = jnp.arange(domains, dtype=jnp.int32)
    home_x = index // DOM_Y
    home_y = index % DOM_Y
    own_slot = jax.random.randint(keys[0], (domains, PAIR_DEV), 0, ORB_DEV)
    step_x = jax.random.randint(keys[1], (domains, PAIR_DEV), -1, 2)
    step_y = jax.random.randint(keys[2], (domains, PAIR_DEV), -1, 2)
    other_slot = jax.random.randint(keys[3], (domains, PAIR_DEV), 0, ORB_DEV)
    other_x = (home_x[:, None] + step_x) % DOM_X
    other_y = (home_y[:, None] + step_y) % DOM_Y
    first = index[:, None] * ORB_DEV + own_slot
    second = (other_x * DOM_Y + other_y) * ORB_DEV + other_slot
    return jnp.stack([first, second], axis=-1).reshape(PAIR_DEV * domains, 2).astype(jnp.int32)


def draw_pair_mask(key, part):
    key = jax.random.fold_in(key, 23)
    keys = jax.random.split(key, 3)
    domains = DOM_X * DOM_Y
    counts = jax.random.randint(keys[0], (domains,), 1, PAIR_DEV + 1)
    fullest = jax.random.randint(keys[1], (), 0, domains)
    counts = jnp.where(jnp.arange(domains) == fullest, PAIR_DEV, counts)
    orders = jax.vmap(lambda k: jax.random.permutation(k, PAIR_DEV))(jax.random.split(keys[2], domains))
    return (orders < counts[:, None]).astype(jnp.int32).reshape(PAIR_DEV * domains)


def plant(drawn, key, low, top_value):
    longest = drawn.shape.index(max(drawn.shape))
    spots = []
    for shift in (0, 1):
        where = [jax.random.randint(jax.random.fold_in(key, axis), (), 0, length) for axis, length in enumerate(drawn.shape)]
        where[longest] = (where[longest] + shift) % drawn.shape[longest]
        spots.append(tuple(where))
    return drawn.at[spots[0]].set(low).at[spots[1]].set(top_value)


def setup_inputs(seed: int = 0) -> dict:
    key_list = jax.random.split(jax.random.key(seed), 5)
    return {
        "orbitals": draw_orbitals(jax.random.fold_in(key_list[4], 71), 0),
        "offsets": plant(jax.random.randint(key_list[1], (ORBS, 3), 0, BOX // 2), jax.random.fold_in(key_list[1], 1), 0, (BOX // 2) - 1).astype(jnp.int32),
        "pair_list": draw_pair_list(jax.random.fold_in(key_list[4], 71), 0),
        "pair_mask": draw_pair_mask(jax.random.fold_in(key_list[4], 71), 0),
    }


def shift_box(field, sx, sy, sz):
    box = field.shape[0]
    flat = field.shape[1]
    padded = jnp.pad(field, ((box, box), (0, 0)))
    field = lax.dynamic_slice_in_dim(padded, (box + sx).astype(jnp.int32), box, 0)
    padded = jnp.pad(field, ((0, 0), (flat, flat)))
    field = lax.dynamic_slice_in_dim(padded, (flat + sy * box).astype(jnp.int32), flat, 1)
    padded = jnp.pad(field, ((0, 0), (box, box)))
    field = lax.dynamic_slice_in_dim(padded, (box + sz).astype(jnp.int32), flat, 1)
    column = jnp.arange(flat, dtype=jnp.int32) % box + sz
    keep = (column >= 0) & (column < box)
    return jnp.where(keep[None, :], field, jnp.zeros_like(field))


def kernel_table(box):
    freq = jnp.arange(box, dtype=jnp.int32)
    freq = freq - box * (freq >= box // 2).astype(jnp.int32)
    wave = (2.0 * math.pi / box) * freq.astype(jnp.float32)
    square = wave * wave
    total = square[:, None, None] + square[None, :, None] + square[None, None, :]
    return 1.0 / (total + (8.0 * math.pi / box) ** 2)


def reference(orbitals, offsets, pair_list, pair_mask):
    box = orbitals.shape[1]
    kernel = kernel_table(box)

    def visit(total, slot):
        first, second, valid = slot
        phi_first = orbitals[first].astype(jnp.float32)
        phi_second = orbitals[second].astype(jnp.float32)
        move = offsets[first] - offsets[second]
        partner = shift_box(phi_second, move[0], move[1], move[2])
        density = phi_first * partner * valid.astype(jnp.float32)
        spectrum = jnp.fft.fftn(density.reshape(box, box, box))
        potential = jnp.real(jnp.fft.ifftn(kernel * spectrum)).astype(jnp.float32).reshape(box, box * box)
        total = total.at[first].add(potential * partner)
        total = total.at[second].add(shift_box(potential * phi_first, -move[0], -move[1], -move[2]))
        return total, None

    start = jnp.zeros(orbitals.shape, jnp.float32)
    total, unused = lax.scan(visit, start, (pair_list[:, 0], pair_list[:, 1], pair_mask))
    return total
```

```python
import functools
import math

import jax
import jax.numpy as jnp
import numpy as np
import ml_dtypes
from jax import lax
from jax.experimental import pallas as pl
from jax.experimental.pallas import tpu as pltpu
from jax.sharding import PartitionSpec as P

BOX = 64
ROW = 96
GROUP = 8
F32 = jnp.float32
BF16 = jnp.bfloat16


def tables():
    n = np.arange(BOX)
    basis = np.zeros((BOX, BOX))
    basis[0] = 1.0
    for m in range(1, BOX // 2):
        basis[2 * m - 1] = math.sqrt(2.0) * np.cos(2.0 * np.pi * m * n / BOX)
        basis[2 * m] = math.sqrt(2.0) * np.sin(2.0 * np.pi * m * n / BOX)
    basis[BOX - 1] = (-1.0) ** n
    basis /= math.sqrt(BOX)

    def cut(value):
        high = value.astype(ml_dtypes.bfloat16)
        low = (value - high.astype(np.float64)).astype(ml_dtypes.bfloat16)
        return high, low

    def right(matrix):
        both = np.kron(np.eye(2), matrix)
        high, low = cut(both)
        half = np.concatenate([high, low], 1)
        return np.concatenate([half, half], 0)

    def left(matrix):
        high, low = cut(matrix)
        return np.concatenate([high, high, low], 1)

    square = (2.0 * np.pi / BOX * ((n + 1) // 2)) ** 2
    some = (2.0 * np.pi / BOX * np.arange(BOX // 2 + 1)) ** 2
    total = some[:, None, None] + square[None, :, None] + np.concatenate([square, square])[None, None, :]
    green = (1.0 / (total + (8.0 * np.pi / BOX) ** 2)).astype(np.float32)
    return right(basis.T), right(basis), left(basis), left(basis.T), green


def split(value):
    high = value.astype(BF16)
    return high, (value - high.astype(F32)).astype(BF16)


def dot(a, b):
    return jnp.dot(a, b, preferred_element_type=F32)


def stacked(first, second):
    return jnp.concatenate([first, second], axis=1)


def kernel(pairs, shift_ref, weight_ref, own_ref, *refs):
    near = refs[: 2 * pairs]
    wz, wzi, rf, ri, green, acc_in, out, held, own, mid = refs[2 * pairs :]
    lanes = 2 * BOX
    low = lax.broadcasted_iota(jnp.int32, (BOX, lanes), 1) < BOX

    row = lax.broadcasted_iota(jnp.int32, (4 * BOX, 4 * BOX), 0)
    col = lax.broadcasted_iota(jnp.int32, (4 * BOX, 4 * BOX), 1)
    row_half, col_half = row // lanes, (col // BOX) % 2
    same = (row_half == col_half) & ((row // BOX) % 2 == col // lanes)
    away = row % BOX - col % BOX

    for y in range(BOX + 1):
        held[pl.ds(y * ROW, ROW - BOX), :] = jnp.zeros((ROW - BOX, lanes), F32)
    held[pl.ds(BOX * ROW, ROW + 32), :] = jnp.zeros((ROW + 32, lanes), F32)

    def own_step(t, _):
        v = own_ref[:, pl.ds(pl.multiple_of(t * lanes, lanes), lanes)].astype(F32)
        r = pltpu.roll(v, BOX, 1)
        base = pl.multiple_of(t * lanes, lanes)
        own[pl.ds(base, BOX), :] = jnp.where(low, v, r)
        own[pl.ds(base + BOX, BOX), :] = jnp.where(low, r, v)
        return 0

    lax.fori_loop(0, BOX // 2, own_step, 0, unroll=4)

    for p in range(pairs):
        a_ref, b_ref = near[2 * p], near[2 * p + 1]
        sx = [shift_ref[3 * (2 * p + h)] for h in range(2)]
        sy = [shift_ref[3 * (2 * p + h) + 1] for h in range(2)]
        sz = [shift_ref[3 * (2 * p + h) + 2] for h in range(2)]
        weight = [weight_ref[2 * p + h] for h in range(2)]

        def solve():
            want = jnp.where(col_half == 0, sz[0], sz[1])
            pick = jnp.where(same & (away == want), 1.0, 0.0).astype(BF16)

            def load_step(t, _):
                at = pl.ds(pl.multiple_of(t * lanes, lanes), lanes)
                v = dot(stacked(a_ref[:, at], b_ref[:, at]), pick)
                base = t * (2 * ROW) + (ROW - BOX)
                held[pl.ds(pl.multiple_of(base, 8), BOX), :] = v[:, :lanes]
                held[pl.ds(pl.multiple_of(base + ROW, 8), BOX), :] = v[:, lanes:]
                return 0

            lax.fori_loop(0, BOX // 2, load_step, 0, unroll=4)

            def partner(y):
                parts = []
                for h in range(2):
                    from_y = y + sy[h]
                    block = jnp.where((from_y >= 0) & (from_y < BOX), from_y, BOX)
                    parts.append(held[pl.ds(block * ROW + (ROW - BOX) + sx[h], BOX), :])
                return jnp.where(low, parts[0], parts[1])

            def forward(i, _):
                rows = []
                for j in range(GROUP):
                    y = i * GROUP + j
                    mine = own[pl.ds(pl.multiple_of(y * BOX, BOX), BOX), :]
                    rows.append(stacked(*split(partner(y) * mine)))
                wave = dot(jnp.concatenate(rows, 0), wz[...])
                high, rest = split(wave[:, :lanes] + wave[:, lanes:])
                for j in range(0, GROUP, 2):
                    at = j * BOX
                    h = stacked(high[at : at + BOX], high[at + BOX : at + 2 * BOX])
                    l = stacked(rest[at : at + BOX], rest[at + BOX : at + 2 * BOX])
                    u = dot(rf[...], jnp.concatenate([h, l, h], 0))
                    y = i * GROUP + j
                    mid[pl.ds(y, BOX, stride=BOX), :] = u[:, :lanes]
                    mid[pl.ds(y + 1, BOX, stride=BOX), :] = u[:, lanes:]
                return 0

            lax.fori_loop(0, BOX // GROUP, forward, 0)

            def middle(i, _):
                for j in range(0, GROUP, 2):
                    k = i * GROUP + j
                    base = pl.multiple_of(k * BOX, BOX)
                    v = stacked(mid[pl.ds(base, BOX), :], mid[pl.ds(base + BOX, BOX), :])
                    h, l = split(v)
                    s = dot(rf[...], jnp.concatenate([h, l, h], 0))
                    s = s * stacked(green[(k + 1) // 2], green[(k + 2) // 2])
                    h, l = split(s)
                    v = dot(ri[...], jnp.concatenate([h, l, h], 0))
                    mid[pl.ds(base, BOX), :] = v[:, :lanes]
                    mid[pl.ds(base + BOX, BOX), :] = v[:, lanes:]
                return 0

            lax.fori_loop(0, BOX // GROUP, middle, 0)

            def backward(i, _):
                rows = []
                for j in range(0, GROUP, 2):
                    y = i * GROUP + j
                    v = stacked(mid[pl.ds(y, BOX, stride=BOX), :], mid[pl.ds(y + 1, BOX, stride=BOX), :])
                    h, l = split(v)
                    u = dot(ri[...], jnp.concatenate([h, l, h], 0))
                    h, l = split(u)
                    rows.append(stacked(h[:, :lanes], l[:, :lanes]))
                    rows.append(stacked(h[:, lanes:], l[:, lanes:]))
                wave = dot(jnp.concatenate(rows, 0), wzi[...])
                field = wave[:, :lanes] + wave[:, lanes:]
                scale = jnp.where(low, weight[0], weight[1])
                for j in range(0, GROUP, 2):
                    y = i * GROUP + j
                    parts = []
                    for k in range(2):
                        v = field[(j + k) * BOX : (j + k + 1) * BOX] * (partner(y + k) * scale)
                        parts.append(v + pltpu.roll(v, BOX, 1))
                    at = pl.ds(pl.multiple_of(y * BOX, lanes), lanes)
                    source = acc_in if p == 0 else out
                    out[:, at] = source[:, at] + jnp.where(low, parts[0], parts[1])
                return 0

            lax.fori_loop(0, BOX // GROUP, backward, 0)

        solve()


def exchange_terms(own, near, shifts, weights, acc):
    pairs = len(near) // 2
    smem = pl.BlockSpec(memory_space=pltpu.SMEM)
    vmem = pl.BlockSpec(memory_space=pltpu.VMEM)
    wz, wzi, rf, ri, green = tables()
    return pl.pallas_call(
        functools.partial(kernel, pairs),
        out_shape=jax.ShapeDtypeStruct((BOX, BOX * BOX), F32),
        in_specs=[smem, smem] + [vmem] * (len(near) + 7),
        out_specs=vmem,
        scratch_shapes=[
            pltpu.VMEM(((BOX + 1) * ROW + 32, 2 * BOX), F32),
            pltpu.VMEM((BOX * BOX, 2 * BOX), F32),
            pltpu.VMEM((BOX * BOX, 2 * BOX), F32),
        ],
        compiler_params=pltpu.CompilerParams(vmem_limit_bytes=48 * 1024 * 1024),
    )(shifts, weights, own, *near, wz, wzi, rf, ri, green, acc)


def shifted(value, axis, steps):
    count = lax.axis_size(axis)
    return lax.ppermute(value, axis, [(i, (i + steps) % count) for i in range(count)])


def body(orbitals, offsets, pair_list, pair_mask):
    count_x, count_y = lax.axis_size("dx"), lax.axis_size("dy")
    place_x, place_y = lax.axis_index("dx"), lax.axis_index("dy")
    mine = place_x * count_y + place_y
    own = orbitals[0]

    owner = pair_list[:, 1]
    rel_x = (owner // count_y - place_x + 1) % count_x
    rel_y = (owner % count_y - place_y + 1) % count_y
    target = rel_x * 3 + rel_y
    used = jnp.where(target[:, None] == jnp.arange(9)[None, :], pair_mask[:, None], 0).sum(0)
    every = lax.all_gather(used, ("dx", "dy"))

    def near(i, j):
        return (place_x + i) % count_x * count_y + (place_y + j) % count_y

    def terms(places, boxes, acc, counts):
        ids = [near(i, j) for i, j in places]
        moves = jnp.concatenate([offsets[mine] - offsets[n] for n in ids])
        return exchange_terms(own, boxes, moves, counts.astype(F32), acc)

    def counts(places):
        return jnp.stack(
            [used[(i + 1) * 3 + j + 1] + every[near(i, j), (1 - i) * 3 + 1 - j] for i, j in places]
        )

    y_up, y_down = shifted(own, "dy", -1), shifted(own, "dy", 1)
    x_up, x_down = shifted(own, "dx", -1), shifted(own, "dx", 1)
    acc = jnp.zeros(own.shape, F32)
    acc = terms([(0, 0)] * 2, [own, own], acc, jnp.stack([used[4], used[4]]))
    places = [(1, 0), (-1, 0)]
    acc = terms(places, [x_up, x_down], acc, counts(places))
    places = [(0, 1), (0, -1)]
    acc = terms(places, [y_up, y_down], acc, counts(places))
    corners = [shifted(y_up, "dx", -1), shifted(y_down, "dx", 1), shifted(y_up, "dx", 1), shifted(y_down, "dx", -1)]
    places = [(1, 1), (-1, -1), (-1, 1), (1, -1)]
    acc = terms(places, corners, acc, counts(places))
    return acc[None]


def solution(mesh):
    placed = (P(("dx", "dy"), None, None), P(), P(("dx", "dy"), None), P(("dx", "dy")))
    return jax.shard_map(
        body, mesh=mesh, in_specs=placed, out_specs=P(("dx", "dy"), None, None), check_vma=False
    )
```

```python
import functools
import math

import jax
import jax.numpy as jnp
import numpy as np
import ml_dtypes
from jax import lax
from jax.experimental import pallas as pl
from jax.experimental.pallas import tpu as pltpu
from jax.sharding import PartitionSpec as P

BOX = 64
ROW = 96
FACTS = 5
MROW = 72
CHUNK = 16
THICK = 8
F32 = jnp.float32
BF16 = jnp.bfloat16


def tables():
    n = np.arange(BOX)
    basis = np.zeros((BOX, BOX))
    basis[0] = 1.0
    for m in range(1, BOX // 2):
        basis[2 * m - 1] = math.sqrt(2.0) * np.cos(2.0 * np.pi * m * n / BOX)
        basis[2 * m] = math.sqrt(2.0) * np.sin(2.0 * np.pi * m * n / BOX)
    basis[BOX - 1] = (-1.0) ** n
    basis /= math.sqrt(BOX)

    def cut(value):
        high = value.astype(ml_dtypes.bfloat16)
        low = (value - high.astype(np.float64)).astype(ml_dtypes.bfloat16)
        return high, low

    def right(matrix):
        both = np.kron(np.eye(2), matrix)
        high, low = cut(both)
        half = np.concatenate([high, low], 1)
        return np.concatenate([half, half], 0)

    def left(matrix):
        high, low = cut(matrix)
        return np.concatenate([high, high, low], 1)

    square = (2.0 * np.pi / BOX * ((n + 1) // 2)) ** 2
    some = (2.0 * np.pi / BOX * np.arange(BOX // 2 + 1)) ** 2
    total = some[:, None, None] + square[None, :, None] + np.concatenate([square, square])[None, None, :]
    green = (1.0 / (total + (8.0 * np.pi / BOX) ** 2)).astype(np.float32)
    return right(basis.T), right(basis), left(basis), left(basis.T), green


def split(value):
    high = value.astype(BF16)
    return high, (value - high.astype(F32)).astype(BF16)


def dot(a, b):
    return jnp.dot(a, b, preferred_element_type=F32)


def stacked(first, second):
    return jnp.concatenate([first, second], axis=1)


def kernel(pairs, info_ref, own_ref, *refs):
    near = refs[: 2 * pairs]
    wz, wzi, rf, ri, green, acc_in, out, held, own, mid, mid2 = refs[2 * pairs :]
    lanes = 2 * BOX
    low = lax.broadcasted_iota(jnp.int32, (BOX, lanes), 1) < BOX

    row = lax.broadcasted_iota(jnp.int32, (4 * BOX, 4 * BOX), 0)
    col = lax.broadcasted_iota(jnp.int32, (4 * BOX, 4 * BOX), 1)
    row_half, col_half = row // lanes, (col // BOX) % 2
    same = (row_half == col_half) & ((row // BOX) % 2 == col // lanes)
    away = row % BOX - col % BOX

    for y in range(BOX + 1):
        held[pl.ds(y * ROW, ROW - BOX), :] = jnp.zeros((ROW - BOX, lanes), F32)
    held[pl.ds(BOX * ROW, ROW + 32), :] = jnp.zeros((ROW + 32, lanes), F32)

    def own_step(t, _):
        v = own_ref[:, pl.ds(pl.multiple_of(t * lanes, lanes), lanes)].astype(F32)
        r = pltpu.roll(v, BOX, 1)
        base = pl.multiple_of(t * lanes, lanes)
        own[pl.ds(base, BOX), :] = jnp.where(low, v, r)
        own[pl.ds(base + BOX, BOX), :] = jnp.where(low, r, v)
        return 0

    lax.fori_loop(0, BOX // 2, own_step, 0, unroll=4)

    for p in range(pairs):
        a_ref, b_ref = near[2 * p], near[2 * p + 1]
        sx, sy, sz, slot, count = [[info_ref[FACTS * (2 * p + h) + f] for h in range(2)] for f in range(FACTS)]

        def weight(ref, h):
            tail = ref[pl.ds(0, 16), pl.ds(BOX * BOX, lanes)].astype(F32)[:8]
            at = lax.broadcasted_iota(jnp.int32, (8, lanes), 1)
            sent = jnp.sum(jnp.where(at == slot[h], tail, 0.0), axis=1, keepdims=True)[:1]
            return sent + count[h].astype(F32)

        def solve():
            want = jnp.where(col_half == 0, sz[0], sz[1])
            pick = jnp.where(same & (away == want), 1.0, 0.0).astype(BF16)

            def load():
                for t0 in range(0, BOX // 2, THICK):
                    rows = []
                    for t in range(t0, t0 + THICK):
                        at = pl.ds(t * lanes, lanes)
                        rows.append(stacked(a_ref[:, at], b_ref[:, at]))
                    v = dot(jnp.concatenate(rows, 0), pick)
                    for t in range(t0, t0 + THICK):
                        base = t * (2 * ROW) + (ROW - BOX)
                        part = v[(t - t0) * BOX : (t - t0 + 1) * BOX]
                        held[pl.ds(base, BOX), :] = part[:, :lanes]
                        held[pl.ds(base + ROW, BOX), :] = part[:, lanes:]

            def partner(y):
                parts = []
                for h in range(2):
                    from_y = y + sy[h]
                    block = jnp.where((from_y >= 0) & (from_y < BOX), from_y, BOX)
                    parts.append(held[pl.ds(block * ROW + (ROW - BOX) + sx[h], BOX), :])
                return jnp.where(low, parts[0], parts[1])

            def skewed(count, first, second):
                before = None
                for c in range(count):
                    now = first(c)
                    if before is not None:
                        second(c - 1, before)
                    before = now
                second(count - 1, before)

            def forward():
                def first(c):
                    rows = []
                    for j in range(CHUNK):
                        y = c * CHUNK + j
                        rows.append(stacked(*split(partner(y) * own[pl.ds(y * BOX, BOX), :])))
                    return dot(jnp.concatenate(rows, 0), wz[...])

                def second(c, wave):
                    high, rest = split(wave[:, :lanes] + wave[:, lanes:])
                    for j in range(0, CHUNK, 2):
                        at = j * BOX
                        h = stacked(high[at : at + BOX], high[at + BOX : at + 2 * BOX])
                        l = stacked(rest[at : at + BOX], rest[at + BOX : at + 2 * BOX])
                        u = dot(rf[...], jnp.concatenate([h, l, h], 0))
                        y = c * CHUNK + j
                        mid[pl.ds(y, BOX, stride=MROW), :] = u[:, :lanes]
                        mid[pl.ds(y + 1, BOX, stride=MROW), :] = u[:, lanes:]

                skewed(BOX // CHUNK, first, second)

            def middle():
                def first(c):
                    waves = []
                    for j in range(0, CHUNK, 2):
                        base = (c * CHUNK + j) * MROW
                        h, l = split(stacked(mid[pl.ds(base, BOX), :], mid[pl.ds(base + MROW, BOX), :]))
                        waves.append(dot(rf[...], jnp.concatenate([h, l, h], 0)))
                    return waves

                def second(c, waves):
                    for j in range(0, CHUNK, 2):
                        k = c * CHUNK + j
                        base = k * MROW
                        h, l = split(waves[j // 2] * stacked(green[(k + 1) // 2], green[(k + 2) // 2]))
                        v = dot(ri[...], jnp.concatenate([h, l, h], 0))
                        mid2[pl.ds(base, BOX), :] = v[:, :lanes]
                        mid2[pl.ds(base + MROW, BOX), :] = v[:, lanes:]

                skewed(BOX // CHUNK, first, second)

            def backward():
                scale = jnp.where(low, weight(a_ref, 0), weight(b_ref, 1))

                def first(c):
                    waves = []
                    for j in range(0, CHUNK, 2):
                        y = c * CHUNK + j
                        v = stacked(mid2[pl.ds(y, BOX, stride=MROW), :], mid2[pl.ds(y + 1, BOX, stride=MROW), :])
                        h, l = split(v)
                        waves.append(dot(ri[...], jnp.concatenate([h, l, h], 0)))
                    return waves

                def second(c, waves):
                    rows = []
                    for u in waves:
                        h, l = split(u)
                        rows.append(stacked(h[:, :lanes], l[:, :lanes]))
                        rows.append(stacked(h[:, lanes:], l[:, lanes:]))
                    wave = dot(jnp.concatenate(rows, 0), wzi[...])
                    field = wave[:, :lanes] + wave[:, lanes:]
                    for j in range(0, CHUNK, 2):
                        y = c * CHUNK + j
                        parts = []
                        for k in range(2):
                            v = field[(j + k) * BOX : (j + k + 1) * BOX] * (partner(y + k) * scale)
                            parts.append(v + pltpu.roll(v, BOX, 1))
                        at = pl.ds(y * BOX, lanes)
                        source = acc_in if p == 0 else out
                        out[:, at] = source[:, at] + jnp.where(low, parts[0], parts[1])

                skewed(BOX // CHUNK, first, second)

            load()
            forward()
            middle()
            backward()

        solve()


def exchange_terms(own, near, info, acc):
    pairs = len(near) // 2
    smem = pl.BlockSpec(memory_space=pltpu.SMEM)
    vmem = pl.BlockSpec(memory_space=pltpu.VMEM)
    wz, wzi, rf, ri, green = tables()
    return pl.pallas_call(
        functools.partial(kernel, pairs),
        out_shape=jax.ShapeDtypeStruct((BOX, BOX * BOX), F32),
        in_specs=[smem] + [vmem] * (len(near) + 7),
        out_specs=vmem,
        scratch_shapes=[
            pltpu.VMEM(((BOX + 1) * ROW + 32, 2 * BOX), F32),
            pltpu.VMEM((BOX * BOX, 2 * BOX), F32),
            pltpu.VMEM((BOX * MROW, 2 * BOX), F32),
            pltpu.VMEM((BOX * MROW, 2 * BOX), F32),
        ],
        compiler_params=pltpu.CompilerParams(vmem_limit_bytes=48 * 1024 * 1024),
    )(info, own, *near, wz, wzi, rf, ri, green, acc)


def body(orbitals, offsets, pair_list, pair_mask):
    count_x, count_y = lax.axis_size("dx"), lax.axis_size("dy")
    place_x, place_y = lax.axis_index("dx"), lax.axis_index("dy")
    mine = place_x * count_y + place_y

    owner = pair_list[:, 1]
    rel_x = (owner // count_y - place_x + 1) % count_x
    rel_y = (owner % count_y - place_y + 1) % count_y
    target = rel_x * 3 + rel_y
    used = jnp.where(target[:, None] == jnp.arange(9)[None, :], pair_mask[:, None], 0).sum(0)
    tail = jnp.broadcast_to(jnp.pad(used, (0, 2 * BOX - 9)).astype(BF16)[None, :], (BOX, 2 * BOX))
    own = jnp.concatenate([orbitals[0], tail], axis=1)

    def facts(places):
        rows = []
        for i, j in places:
            other = (place_x + i) % count_x * count_y + (place_y + j) % count_y
            move = offsets[mine] - offsets[other]
            ends = jnp.stack([(1 - i) * 3 + 1 - j, used[(1 + i) * 3 + 1 + j]])
            rows.append(jnp.concatenate([move, ends]))
        return jnp.concatenate(rows).astype(jnp.int32)

    def along(value, axis, to):
        return lax.ppermute(value, axis, [(i, to(i)) for i in range(lax.axis_size(axis))])

    inner = lambda i: i ^ 1
    outer = lambda i: ((i + 1) ^ 1) - 1 if 0 < i < count_x - 1 else count_x - 1 - i
    near = 1 - 2 * (place_x % 2)
    far = -near

    y_next = along(own, "dy", lambda i: (i - 1) % count_y)
    y_last = along(own, "dy", lambda i: (i + 1) % count_y)
    x_near, x_far = along(own, "dx", inner), along(own, "dx", outer)
    acc = jnp.zeros((BOX, BOX * BOX), F32)
    acc = exchange_terms(own, [own, own], facts([(0, 0), (0, 0)]) * jnp.array([1, 1, 1, 1, 0] * 2), acc)
    acc = exchange_terms(own, [x_near, x_far], facts([(near, 0), (far, 0)]), acc)
    corners = [along(v, "dx", to) for to in (inner, outer) for v in (y_next, y_last)]
    acc = exchange_terms(own, [y_next, y_last], facts([(0, 1), (0, -1)]), acc)
    acc = exchange_terms(own, corners[:2], facts([(near, 1), (near, -1)]), acc)
    acc = exchange_terms(own, corners[2:], facts([(far, 1), (far, -1)]), acc)
    return acc[None]


def solution(mesh):
    placed = (P(("dx", "dy"), None, None), P(), P(("dx", "dy"), None), P(("dx", "dy")))
    return jax.shard_map(
        body, mesh=mesh, in_specs=placed, out_specs=P(("dx", "dy"), None, None), check_vma=False
    )
```

```python
import functools
import math

import jax
import jax.numpy as jnp
import numpy as np
import ml_dtypes
from jax import lax
from jax.experimental import pallas as pl
from jax.experimental.pallas import tpu as pltpu
from jax.sharding import PartitionSpec as P

BOX = 64
ROW = 96
HOME = (0, 0)
MROW = 72
CHUNK = 16
THICK = 8
F32 = jnp.float32
BF16 = jnp.bfloat16


def tables():
    n = np.arange(BOX)
    basis = np.zeros((BOX, BOX))
    basis[0] = 1.0
    for m in range(1, BOX // 2):
        basis[2 * m - 1] = math.sqrt(2.0) * np.cos(2.0 * np.pi * m * n / BOX)
        basis[2 * m] = math.sqrt(2.0) * np.sin(2.0 * np.pi * m * n / BOX)
    basis[BOX - 1] = (-1.0) ** n
    basis /= math.sqrt(BOX)

    def cut(value):
        high = value.astype(ml_dtypes.bfloat16)
        low = (value - high.astype(np.float64)).astype(ml_dtypes.bfloat16)
        return high, low

    def right(matrix):
        both = np.kron(np.eye(2), matrix)
        high, low = cut(both)
        half = np.concatenate([high, low], 1)
        return np.concatenate([half, half], 0)

    def left(matrix):
        high, low = cut(matrix)
        return np.concatenate([high, high, low], 1)

    square = (2.0 * np.pi / BOX * ((n + 1) // 2)) ** 2
    some = (2.0 * np.pi / BOX * np.arange(BOX // 2 + 1)) ** 2
    total = some[:, None, None] + square[None, :, None] + np.concatenate([square, square])[None, None, :]
    green = (1.0 / (total + (8.0 * np.pi / BOX) ** 2)).astype(np.float32)
    return right(basis.T), right(basis), left(basis), left(basis.T), green


def split(value):
    high = value.astype(BF16)
    return high, (value - high.astype(F32)).astype(BF16)


def dot(a, b):
    return jnp.dot(a, b, preferred_element_type=F32)


def stacked(first, second):
    return jnp.concatenate([first, second], axis=1)


def target(pair_list, slot):
    size_x, size_y = lax.axis_size("dx"), lax.axis_size("dy")
    owner = pair_list[slot, 1]
    rel_x = (owner // size_y - lax.axis_index("dx") + 1 + size_x) % size_x
    rel_y = (owner % size_y - lax.axis_index("dy") + 1 + size_y) % size_y
    return rel_x * 3 + rel_y


def known(i, j, offsets, pair_list, pair_mask):
    size_x, size_y = lax.axis_size("dx"), lax.axis_size("dy")
    here_x, here_y = lax.axis_index("dx"), lax.axis_index("dy")
    if (i, j) == HOME:
        return tuple(0 * offsets[0, c] for c in range(3)) + (4 + 0 * offsets[0, 0], 0 * offsets[0, 0])
    step = i * (1 - 2 * (here_x % 2))
    other = (here_x + step + size_x) % size_x * size_y + (here_y + j + size_y) % size_y
    mine = here_x * size_y + here_y
    move = tuple(offsets[mine, c] - offsets[other, c] for c in range(3))
    index = (1 + step) * 3 + 1 + j
    count = sum(jnp.where(target(pair_list, n) == index, pair_mask[n], 0) for n in range(pair_list.shape[0]))
    return move + (8 - index, count)


def tail_kernel(pair_list, pair_mask, box, out):
    lane = lax.broadcasted_iota(jnp.int32, (BOX, 2 * BOX), 1)
    counts = jnp.zeros((BOX, 2 * BOX), jnp.int32)
    for n in range(pair_list.shape[0]):
        counts += jnp.where(lane == target(pair_list, n), pair_mask[n], 0)
    out[:, pl.ds(BOX * BOX, 2 * BOX)] = counts.astype(F32).astype(BF16)
    out[:, pl.ds(0, BOX * BOX)] = box[...]


def kernel(places, offsets, pair_list, pair_mask, own_ref, *refs):
    pairs = len(places) // 2
    near = refs[: 2 * pairs]
    if places[0] == HOME:
        wz, wzi, rf, ri, green, out, own, held, mid, mid2 = refs[2 * pairs :]
        acc_in = None
    else:
        wz, wzi, rf, ri, green, acc_in, out, held, mid, mid2 = refs[2 * pairs :]
        own = own_ref
    facts = [known(i, j, offsets, pair_list, pair_mask) for i, j in places]
    lanes = 2 * BOX
    low = lax.broadcasted_iota(jnp.int32, (BOX, lanes), 1) < BOX

    row = lax.broadcasted_iota(jnp.int32, (4 * BOX, 4 * BOX), 0)
    col = lax.broadcasted_iota(jnp.int32, (4 * BOX, 4 * BOX), 1)
    row_half, col_half = row // lanes, (col // BOX) % 2
    same = (row_half == col_half) & ((row // BOX) % 2 == col // lanes)
    away = row % BOX - col % BOX

    for y in range(BOX + 1):
        held[pl.ds(y * ROW, ROW - BOX), :] = jnp.zeros((ROW - BOX, lanes), F32)
    held[pl.ds(BOX * ROW, ROW + 32), :] = jnp.zeros((ROW + 32, lanes), F32)

    def own_step(t, _):
        v = own_ref[:, pl.ds(pl.multiple_of(t * lanes, lanes), lanes)].astype(F32)
        r = pltpu.roll(v, BOX, 1)
        base = pl.multiple_of(t * lanes, lanes)
        own[pl.ds(base, BOX), :] = jnp.where(low, v, r)
        own[pl.ds(base + BOX, BOX), :] = jnp.where(low, r, v)
        return 0

    if places[0] == HOME:
        lax.fori_loop(0, BOX // 2, own_step, 0, unroll=4)

    for p in range(pairs):
        a_ref, b_ref = near[2 * p], near[2 * p + 1]
        sx, sy, sz, slot, count = zip(*facts[2 * p : 2 * p + 2])

        def weight(ref, h):
            tail = ref[pl.ds(0, 16), pl.ds(BOX * BOX, lanes)].astype(F32)[:8]
            at = lax.broadcasted_iota(jnp.int32, (8, lanes), 1)
            sent = jnp.sum(jnp.where(at == slot[h], tail, 0.0), axis=1, keepdims=True)[:1]
            return sent + count[h].astype(F32)

        def solve():
            want = jnp.where(col_half == 0, sz[0], sz[1])
            pick = jnp.where(same & (away == want), 1.0, 0.0).astype(BF16)

            def load():
                for t0 in range(0, BOX // 2, THICK):
                    rows = []
                    for t in range(t0, t0 + THICK):
                        at = pl.ds(t * lanes, lanes)
                        rows.append(stacked(a_ref[:, at], b_ref[:, at]))
                    v = dot(jnp.concatenate(rows, 0), pick)
                    for t in range(t0, t0 + THICK):
                        base = t * (2 * ROW) + (ROW - BOX)
                        part = v[(t - t0) * BOX : (t - t0 + 1) * BOX]
                        held[pl.ds(base, BOX), :] = part[:, :lanes]
                        held[pl.ds(base + ROW, BOX), :] = part[:, lanes:]

            def partner(y):
                parts = []
                for h in range(2):
                    from_y = y + sy[h]
                    block = jnp.where((from_y >= 0) & (from_y < BOX), from_y, BOX)
                    parts.append(held[pl.ds(block * ROW + (ROW - BOX) + sx[h], BOX), :])
                return jnp.where(low, parts[0], parts[1])

            def skewed(count, first, second):
                before = None
                for c in range(count):
                    now = first(c)
                    if before is not None:
                        second(c - 1, before)
                    before = now
                second(count - 1, before)

            def forward():
                def first(c):
                    rows = []
                    for j in range(CHUNK):
                        y = c * CHUNK + j
                        rows.append(stacked(*split(partner(y) * own[pl.ds(y * BOX, BOX), :])))
                    return dot(jnp.concatenate(rows, 0), wz[...])

                def second(c, wave):
                    high, rest = split(wave[:, :lanes] + wave[:, lanes:])
                    for j in range(0, CHUNK, 2):
                        at = j * BOX
                        h = stacked(high[at : at + BOX], high[at + BOX : at + 2 * BOX])
                        l = stacked(rest[at : at + BOX], rest[at + BOX : at + 2 * BOX])
                        u = dot(rf[...], jnp.concatenate([h, l, h], 0))
                        y = c * CHUNK + j
                        mid[pl.ds(y, BOX, stride=MROW), :] = u[:, :lanes]
                        mid[pl.ds(y + 1, BOX, stride=MROW), :] = u[:, lanes:]

                skewed(BOX // CHUNK, first, second)

            def middle():
                def first(c):
                    waves = []
                    for j in range(0, CHUNK, 2):
                        base = (c * CHUNK + j) * MROW
                        h, l = split(stacked(mid[pl.ds(base, BOX), :], mid[pl.ds(base + MROW, BOX), :]))
                        waves.append(dot(rf[...], jnp.concatenate([h, l, h], 0)))
                    return waves

                def second(c, waves):
                    for j in range(0, CHUNK, 2):
                        k = c * CHUNK + j
                        base = k * MROW
                        h, l = split(waves[j // 2] * stacked(green[(k + 1) // 2], green[(k + 2) // 2]))
                        v = dot(ri[...], jnp.concatenate([h, l, h], 0))
                        mid2[pl.ds(base, BOX), :] = v[:, :lanes]
                        mid2[pl.ds(base + MROW, BOX), :] = v[:, lanes:]

                skewed(BOX // CHUNK, first, second)

            def backward():
                scale = jnp.where(low, weight(a_ref, 0), weight(b_ref, 1))

                def first(c):
                    waves = []
                    for j in range(0, CHUNK, 2):
                        y = c * CHUNK + j
                        v = stacked(mid2[pl.ds(y, BOX, stride=MROW), :], mid2[pl.ds(y + 1, BOX, stride=MROW), :])
                        h, l = split(v)
                        waves.append(dot(ri[...], jnp.concatenate([h, l, h], 0)))
                    return waves

                def second(c, waves):
                    rows = []
                    for u in waves:
                        h, l = split(u)
                        rows.append(stacked(h[:, :lanes], l[:, :lanes]))
                        rows.append(stacked(h[:, lanes:], l[:, lanes:]))
                    wave = dot(jnp.concatenate(rows, 0), wzi[...])
                    field = wave[:, :lanes] + wave[:, lanes:]
                    for j in range(0, CHUNK, 2):
                        y = c * CHUNK + j
                        parts = []
                        for k in range(2):
                            v = field[(j + k) * BOX : (j + k + 1) * BOX] * (partner(y + k) * scale)
                            parts.append(v + pltpu.roll(v, BOX, 1))
                        at = pl.ds(y * BOX, lanes)
                        both = jnp.where(low, parts[0], parts[1])
                        if p > 0:
                            both = out[:, at] + both
                        elif acc_in is not None:
                            both = acc_in[:, at] + both
                        out[:, at] = both

                skewed(BOX // CHUNK, first, second)

            load()
            forward()
            middle()
            backward()

        solve()


SMEM = pl.BlockSpec(memory_space=pltpu.SMEM)
VMEM = pl.BlockSpec(memory_space=pltpu.VMEM)
PARAMS = pltpu.CompilerParams(vmem_limit_bytes=48 * 1024 * 1024)


def exchange_terms(places, ints, own, boxes, *acc):
    first = places[0] == HOME
    shape = [jax.ShapeDtypeStruct((BOX, BOX * BOX), F32)]
    if first:
        shape.append(jax.ShapeDtypeStruct((BOX * BOX, 2 * BOX), F32))
    return pl.pallas_call(
        functools.partial(kernel, places),
        out_shape=shape,
        in_specs=[SMEM] * 3 + [VMEM] * (len(boxes) + 6 + len(acc)),
        out_specs=[VMEM] * len(shape),
        scratch_shapes=[
            pltpu.VMEM(((BOX + 1) * ROW + 32, 2 * BOX), F32),
            pltpu.VMEM((BOX * MROW, 2 * BOX), F32),
            pltpu.VMEM((BOX * MROW, 2 * BOX), F32),
        ],
        compiler_params=PARAMS,
    )(*ints, own, *boxes, *tables(), *acc)


def along(value, axis, to):
    return lax.ppermute(value, axis, [(i, to(i)) for i in range(lax.axis_size(axis))])


def body(orbitals, offsets, pair_list, pair_mask):
    size_x, size_y = lax.axis_size("dx"), lax.axis_size("dy")
    ints = (offsets, pair_list, pair_mask)
    own = pl.pallas_call(
        tail_kernel,
        out_shape=jax.ShapeDtypeStruct((BOX, BOX * BOX + 2 * BOX), BF16),
        in_specs=[SMEM, SMEM, VMEM],
        out_specs=VMEM,
        compiler_params=PARAMS,
    )(pair_list, pair_mask, orbitals[0])

    def inner(i):
        return i ^ 1

    def outer(i):
        return (i - 1 + 2 * (i % 2)) % size_x

    y_next = along(own, "dy", lambda i: (i - 1) % size_y)
    y_last = along(own, "dy", lambda i: (i + 1) % size_y)
    x_near, x_far = along(own, "dx", inner), along(own, "dx", outer)
    acc, wide = exchange_terms((HOME, HOME), ints, own, (own, own))
    (acc,) = exchange_terms(((1, 0), (-1, 0)), ints, wide, (x_near, x_far), acc)
    y_next, y_last, acc = lax.optimization_barrier((y_next, y_last, acc))
    corners = [along(v, "dx", to) for to in (inner, outer) for v in (y_next, y_last)]
    (acc,) = exchange_terms(((0, 1), (0, -1)), ints, wide, (y_next, y_last), acc)
    (acc,) = exchange_terms(((1, 1), (1, -1)), ints, wide, corners[:2], acc)
    (acc,) = exchange_terms(((-1, 1), (-1, -1)), ints, wide, corners[2:], acc)
    return acc[None]


def solution(mesh):
    placed = (P(("dx", "dy"), None, None), P(), P(("dx", "dy"), None), P(("dx", "dy")))
    return jax.shard_map(
        body, mesh=mesh, in_specs=placed, out_specs=P(("dx", "dy"), None, None), check_vma=False
    )
```

```python
import functools
import math

import jax
import jax.numpy as jnp
import numpy as np
import ml_dtypes
from jax import lax
from jax.experimental import pallas as pl
from jax.experimental.pallas import tpu as pltpu
from jax.sharding import PartitionSpec as P

BOX = 64
ROW = 96
HOME = (0, 0)
GREEN = (BOX // 2 + 1) * BOX
MROW = 72
CHUNK = 16
THICK = 8
F32 = jnp.float32
BF16 = jnp.bfloat16


def tables():
    n = np.arange(BOX)
    basis = np.zeros((BOX, BOX))
    basis[0] = 1.0
    for m in range(1, BOX // 2):
        basis[2 * m - 1] = math.sqrt(2.0) * np.cos(2.0 * np.pi * m * n / BOX)
        basis[2 * m] = math.sqrt(2.0) * np.sin(2.0 * np.pi * m * n / BOX)
    basis[BOX - 1] = (-1.0) ** n
    basis /= math.sqrt(BOX)

    def cut(value):
        high = value.astype(ml_dtypes.bfloat16)
        low = (value - high.astype(np.float64)).astype(ml_dtypes.bfloat16)
        return high, low

    def right(matrix):
        both = np.kron(np.eye(2), matrix)
        high, low = cut(both)
        half = np.concatenate([high, low], 1)
        return np.concatenate([half, half], 0)

    def left(matrix):
        high, low = cut(matrix)
        return np.concatenate([high, high, low], 1)

    square = (2.0 * np.pi / BOX * ((n + 1) // 2)) ** 2
    some = (2.0 * np.pi / BOX * np.arange(BOX // 2 + 1)) ** 2
    total = some[:, None, None] + square[None, :, None] + np.concatenate([square, square])[None, None, :]
    green = (1.0 / (total + (8.0 * np.pi / BOX) ** 2)).astype(np.float32)
    blocks = [green.reshape(-1, 2 * BOX)]
    for wide in (right(basis.T), right(basis), left(basis), left(basis.T)):
        wide = np.pad(wide.astype(np.float32), ((0, 0), (0, 4 * BOX - wide.shape[1])))
        blocks += [wide[:, : 2 * BOX], wide[:, 2 * BOX :]]
    return np.concatenate(blocks, 0)


def split(value):
    high = value.astype(BF16)
    return high, (value - high.astype(F32)).astype(BF16)


def dot(a, b):
    return jnp.dot(a, b, preferred_element_type=F32)


def stacked(first, second):
    return jnp.concatenate([first, second], axis=1)


def target(pair_list, slot):
    size_x, size_y = lax.axis_size("dx"), lax.axis_size("dy")
    owner = pair_list[1, slot]
    rel_x = (owner // size_y - lax.axis_index("dx") + 1 + size_x) % size_x
    rel_y = (owner % size_y - lax.axis_index("dy") + 1 + size_y) % size_y
    return rel_x * 3 + rel_y


def known(i, j, offsets, pair_list, pair_mask):
    size_x, size_y = lax.axis_size("dx"), lax.axis_size("dy")
    here_x, here_y = lax.axis_index("dx"), lax.axis_index("dy")
    if (i, j) == HOME:
        return tuple(0 * offsets[c, 0] for c in range(3)) + (4 + 0 * offsets[0, 0], 0 * offsets[0, 0])
    step = i * (1 - 2 * (here_x % 2))
    other = (here_x + step + size_x) % size_x * size_y + (here_y + j + size_y) % size_y
    mine = here_x * size_y + here_y
    move = tuple(offsets[c, mine] - offsets[c, other] for c in range(3))
    index = (1 + step) * 3 + 1 + j
    count = sum(jnp.where(target(pair_list, n) == index, pair_mask[n], 0) for n in range(pair_list.shape[1]))
    return move + (8 - index, count)


def tail_kernel(list_hbm, mask_hbm, box_hbm, out, pair_list, pair_mask, sems):
    copies = [
        pltpu.make_async_copy(box_hbm, out.at[:, pl.ds(0, BOX * BOX)], sems.at[0]),
        pltpu.make_async_copy(list_hbm, pair_list, sems.at[1]),
        pltpu.make_async_copy(mask_hbm, pair_mask, sems.at[2]),
    ]
    for copy in copies:
        copy.start()
    copies[1].wait()
    copies[2].wait()
    lane = lax.broadcasted_iota(jnp.int32, (BOX, 2 * BOX), 1)
    counts = jnp.zeros((BOX, 2 * BOX), jnp.int32)
    for n in range(pair_list.shape[1]):
        counts += jnp.where(lane == target(pair_list, n), pair_mask[n], 0)
    out[:, pl.ds(BOX * BOX, 2 * BOX)] = counts.astype(F32).astype(BF16)
    copies[0].wait()


def kernel(places, last, offsets, pair_list, pair_mask, own_ref, *refs):
    pairs = len(places) // 2
    near, (tab_hbm, *refs) = refs[: 2 * pairs], refs[2 * pairs :]
    acc_in = None
    if places[0] == HOME:
        out, own, *refs = refs
    else:
        acc_in, out, *refs = refs
        own = own_ref
    if last:
        out_hbm, (out, out_sem, *refs) = out, refs
    held, mid, mid2, tab, wz, wzi, rf, ri, tab_sem = refs
    tab_copy = pltpu.make_async_copy(tab_hbm, tab, tab_sem)
    tab_copy.start()
    facts = [known(i, j, offsets, pair_list, pair_mask) for i, j in places]
    lanes = 2 * BOX
    low = lax.broadcasted_iota(jnp.int32, (BOX, lanes), 1) < BOX

    row = lax.broadcasted_iota(jnp.int32, (4 * BOX, 4 * BOX), 0)
    col = lax.broadcasted_iota(jnp.int32, (4 * BOX, 4 * BOX), 1)
    row_half, col_half = row // lanes, (col // BOX) % 2
    same = (row_half == col_half) & ((row // BOX) % 2 == col // lanes)
    away = row % BOX - col % BOX

    for y in range(BOX + 1):
        held[pl.ds(y * ROW, ROW - BOX), :] = jnp.zeros((ROW - BOX, lanes), F32)
    held[pl.ds(BOX * ROW, ROW + 32), :] = jnp.zeros((ROW + 32, lanes), F32)

    def own_step(t, _):
        v = own_ref[:, pl.ds(pl.multiple_of(t * lanes, lanes), lanes)].astype(F32)
        r = pltpu.roll(v, BOX, 1)
        base = pl.multiple_of(t * lanes, lanes)
        own[pl.ds(base, BOX), :] = jnp.where(low, v, r)
        own[pl.ds(base + BOX, BOX), :] = jnp.where(low, r, v)
        return 0

    if places[0] == HOME:
        lax.fori_loop(0, BOX // 2, own_step, 0, unroll=4)

    def out_copy(c):
        at = pl.ds(c * CHUNK * BOX, CHUNK * BOX)
        return pltpu.make_async_copy(out.at[:, at], out_hbm.at[:, at], out_sem.at[c])

    def ready():
        tab_copy.wait()
        at = GREEN
        for ref in (wz, wzi, rf, ri):
            size, width = ref.shape
            ref[:, pl.ds(0, lanes)] = tab[pl.ds(at, size), :].astype(BF16)
            ref[:, pl.ds(lanes, width - lanes)] = tab[pl.ds(at + size, size), :][:, : width - lanes].astype(BF16)
            at += 2 * size

    for p in range(pairs):
        a_ref, b_ref = near[2 * p], near[2 * p + 1]
        sx, sy, sz, slot, count = zip(*facts[2 * p : 2 * p + 2])

        def weight(ref, h):
            tail = ref[pl.ds(0, 16), pl.ds(BOX * BOX, lanes)].astype(F32)[:8]
            at = lax.broadcasted_iota(jnp.int32, (8, lanes), 1)
            sent = jnp.sum(jnp.where(at == slot[h], tail, 0.0), axis=1, keepdims=True)[:1]
            return sent + count[h].astype(F32)

        def solve():
            want = jnp.where(col_half == 0, sz[0], sz[1])
            pick = jnp.where(same & (away == want), 1.0, 0.0).astype(BF16)

            def load():
                for t0 in range(0, BOX // 2, THICK):
                    rows = []
                    for t in range(t0, t0 + THICK):
                        at = pl.ds(t * lanes, lanes)
                        rows.append(stacked(a_ref[:, at], b_ref[:, at]))
                    v = dot(jnp.concatenate(rows, 0), pick)
                    for t in range(t0, t0 + THICK):
                        base = t * (2 * ROW) + (ROW - BOX)
                        part = v[(t - t0) * BOX : (t - t0 + 1) * BOX]
                        held[pl.ds(base, BOX), :] = part[:, :lanes]
                        held[pl.ds(base + ROW, BOX), :] = part[:, lanes:]

            def partner(y):
                parts = []
                for h in range(2):
                    from_y = y + sy[h]
                    block = jnp.where((from_y >= 0) & (from_y < BOX), from_y, BOX)
                    parts.append(held[pl.ds(block * ROW + (ROW - BOX) + sx[h], BOX), :])
                return jnp.where(low, parts[0], parts[1])

            def skewed(count, first, second):
                before = None
                for c in range(count):
                    now = first(c)
                    if before is not None:
                        second(c - 1, before)
                    before = now
                second(count - 1, before)

            def forward():
                def first(c):
                    rows = []
                    for j in range(CHUNK):
                        y = c * CHUNK + j
                        rows.append(stacked(*split(partner(y) * own[pl.ds(y * BOX, BOX), :])))
                    return dot(jnp.concatenate(rows, 0), wz[...])

                def second(c, wave):
                    high, rest = split(wave[:, :lanes] + wave[:, lanes:])
                    for j in range(0, CHUNK, 2):
                        at = j * BOX
                        h = stacked(high[at : at + BOX], high[at + BOX : at + 2 * BOX])
                        l = stacked(rest[at : at + BOX], rest[at + BOX : at + 2 * BOX])
                        u = dot(rf[...], jnp.concatenate([h, l, h], 0))
                        y = c * CHUNK + j
                        mid[pl.ds(y, BOX, stride=MROW), :] = u[:, :lanes]
                        mid[pl.ds(y + 1, BOX, stride=MROW), :] = u[:, lanes:]

                skewed(BOX // CHUNK, first, second)

            def green(k):
                return tab[pl.ds(k * BOX, BOX), :]

            def middle():
                def first(c):
                    waves = []
                    for j in range(0, CHUNK, 2):
                        base = (c * CHUNK + j) * MROW
                        h, l = split(stacked(mid[pl.ds(base, BOX), :], mid[pl.ds(base + MROW, BOX), :]))
                        waves.append(dot(rf[...], jnp.concatenate([h, l, h], 0)))
                    return waves

                def second(c, waves):
                    for j in range(0, CHUNK, 2):
                        k = c * CHUNK + j
                        base = k * MROW
                        h, l = split(waves[j // 2] * stacked(green((k + 1) // 2), green((k + 2) // 2)))
                        v = dot(ri[...], jnp.concatenate([h, l, h], 0))
                        mid2[pl.ds(base, BOX), :] = v[:, :lanes]
                        mid2[pl.ds(base + MROW, BOX), :] = v[:, lanes:]

                skewed(BOX // CHUNK, first, second)

            def backward():
                scale = jnp.where(low, weight(a_ref, 0), weight(b_ref, 1))

                def first(c):
                    waves = []
                    for j in range(0, CHUNK, 2):
                        y = c * CHUNK + j
                        v = stacked(mid2[pl.ds(y, BOX, stride=MROW), :], mid2[pl.ds(y + 1, BOX, stride=MROW), :])
                        h, l = split(v)
                        waves.append(dot(ri[...], jnp.concatenate([h, l, h], 0)))
                    return waves

                def second(c, waves):
                    rows = []
                    for u in waves:
                        h, l = split(u)
                        rows.append(stacked(h[:, :lanes], l[:, :lanes]))
                        rows.append(stacked(h[:, lanes:], l[:, lanes:]))
                    wave = dot(jnp.concatenate(rows, 0), wzi[...])
                    field = wave[:, :lanes] + wave[:, lanes:]
                    for j in range(0, CHUNK, 2):
                        y = c * CHUNK + j
                        parts = []
                        for k in range(2):
                            v = field[(j + k) * BOX : (j + k + 1) * BOX] * (partner(y + k) * scale)
                            parts.append(v + pltpu.roll(v, BOX, 1))
                        at = pl.ds(y * BOX, lanes)
                        both = jnp.where(low, parts[0], parts[1])
                        if p > 0:
                            both = out[:, at] + both
                        elif acc_in is not None:
                            both = acc_in[:, at] + both
                        out[:, at] = both
                    if last and p == pairs - 1:
                        out_copy(c).start()

                skewed(BOX // CHUNK, first, second)

            load()
            if p == 0:
                ready()
            forward()
            middle()
            backward()

        solve()

    if last:
        for c in range(BOX // CHUNK):
            out_copy(c).wait()


SMEM = pl.BlockSpec(memory_space=pltpu.SMEM)
HBM = pl.BlockSpec(memory_space=pltpu.HBM)
VMEM = pl.BlockSpec(memory_space=pltpu.VMEM)
PARAMS = pltpu.CompilerParams(vmem_limit_bytes=28 * 1024 * 1024)


def exchange_terms(places, ints, own, boxes, *acc, last=False):
    lanes = 2 * BOX
    shape = [jax.ShapeDtypeStruct((BOX, BOX * BOX), F32)]
    if places[0] == HOME:
        shape.append(jax.ShapeDtypeStruct((BOX * BOX, lanes), F32))
    sink = [pltpu.VMEM((BOX, BOX * BOX), F32), pltpu.SemaphoreType.DMA((BOX // CHUNK,))] if last else []
    table = tables()
    return pl.pallas_call(
        functools.partial(kernel, places, last),
        out_shape=shape,
        in_specs=[SMEM] * 3 + [VMEM] * (1 + len(boxes)) + [HBM] + [VMEM] * len(acc),
        out_specs=[HBM if last else VMEM] * len(shape),
        scratch_shapes=sink
        + [
            pltpu.VMEM(((BOX + 1) * ROW + 32, lanes), F32),
            pltpu.VMEM((BOX * MROW, lanes), F32),
            pltpu.VMEM((BOX * MROW, lanes), F32),
            pltpu.VMEM(table.shape, F32),
            pltpu.VMEM((2 * lanes, 2 * lanes), BF16),
            pltpu.VMEM((2 * lanes, 2 * lanes), BF16),
            pltpu.VMEM((BOX, 3 * BOX), BF16),
            pltpu.VMEM((BOX, 3 * BOX), BF16),
            pltpu.SemaphoreType.DMA,
        ],
        compiler_params=PARAMS,
    )(*ints, own, *boxes, table, *acc)


def along(value, axis, to):
    return lax.ppermute(value, axis, [(i, to(i)) for i in range(lax.axis_size(axis))])


def body(orbitals, offsets, pair_list, pair_mask):
    size_x, size_y = lax.axis_size("dx"), lax.axis_size("dy")
    ints = (offsets.T, pair_list.T, pair_mask)
    own = pl.pallas_call(
        tail_kernel,
        out_shape=jax.ShapeDtypeStruct((BOX, BOX * BOX + 2 * BOX), BF16),
        in_specs=[HBM] * 3,
        out_specs=VMEM,
        scratch_shapes=[
            pltpu.SMEM(ints[1].shape, jnp.int32),
            pltpu.SMEM(pair_mask.shape, jnp.int32),
            pltpu.SemaphoreType.DMA((3,)),
        ],
        compiler_params=PARAMS,
    )(ints[1], pair_mask, orbitals[0])

    def inner(i):
        return i ^ 1

    def outer(i):
        return (i - 1 + 2 * (i % 2)) % size_x

    y_next = along(own, "dy", lambda i: (i - 1) % size_y)
    y_last = along(own, "dy", lambda i: (i + 1) % size_y)
    x_near, x_far = along(own, "dx", inner), along(own, "dx", outer)
    acc, wide = exchange_terms((HOME, HOME), ints, own, (own, own))
    (acc,) = exchange_terms(((1, 0), (-1, 0)), ints, wide, (x_near, x_far), acc)
    y_next, y_last, acc = lax.optimization_barrier((y_next, y_last, acc))
    corners = [along(v, "dx", to) for to in (inner, outer) for v in (y_next, y_last)]
    (acc,) = exchange_terms(((0, 1), (0, -1)), ints, wide, (y_next, y_last), acc)
    (acc,) = exchange_terms(((1, 1), (1, -1)), ints, wide, corners[:2], acc)
    (acc,) = exchange_terms(((-1, 1), (-1, -1)), ints, wide, corners[2:], acc, last=True)
    return acc[None]


def solution(mesh):
    placed = (P(("dx", "dy"), None, None), P(), P(("dx", "dy"), None), P(("dx", "dy")))
    return jax.shard_map(
        body, mesh=mesh, in_specs=placed, out_specs=P(("dx", "dy"), None, None), check_vma=False
    )
```

```python
import functools
import math

import jax
import jax.numpy as jnp
import numpy as np
import ml_dtypes
from jax import lax
from jax.experimental import pallas as pl
from jax.experimental.pallas import tpu as pltpu
from jax.sharding import PartitionSpec as P

BOX = 64
ROW = 96
GREEN = (BOX // 2 + 1) * BOX
MROW = 72
HROW = 40
CHUNK = 16
THICK = 8
F32 = jnp.float32
BF16 = jnp.bfloat16


def tables():
    n = np.arange(BOX)
    basis = np.zeros((BOX, BOX))
    basis[0] = 1.0
    for m in range(1, BOX // 2):
        basis[2 * m - 1] = math.sqrt(2.0) * np.cos(2.0 * np.pi * m * n / BOX)
        basis[2 * m] = math.sqrt(2.0) * np.sin(2.0 * np.pi * m * n / BOX)
    basis[BOX - 1] = (-1.0) ** n
    basis /= math.sqrt(BOX)

    def cut(value):
        high = value.astype(ml_dtypes.bfloat16)
        low = (value - high.astype(np.float64)).astype(ml_dtypes.bfloat16)
        return high, low

    def right(matrix):
        both = np.kron(np.eye(2), matrix)
        high, low = cut(both)
        half = np.concatenate([high, low], 1)
        return np.concatenate([half, half], 0)

    def left(matrix):
        high, low = cut(matrix)
        return np.concatenate([high, high, low], 1)

    square = (2.0 * np.pi / BOX * ((n + 1) // 2)) ** 2
    some = (2.0 * np.pi / BOX * np.arange(BOX // 2 + 1)) ** 2
    total = some[:, None, None] + square[None, :, None] + np.concatenate([square, square])[None, None, :]
    green = (1.0 / (total + (8.0 * np.pi / BOX) ** 2)).astype(np.float32)
    def packed(first, *tables):
        blocks = [first.reshape(-1, 2 * BOX)]
        for wide in tables:
            wide = np.pad(wide.astype(np.float32), ((0, 0), (0, 4 * BOX - wide.shape[1])))
            blocks += [wide[:, : 2 * BOX], wide[:, 2 * BOX :]]
        return np.concatenate(blocks, 0)

    four = (right(basis.T), right(basis), left(basis), left(basis.T))
    even = [m for m in range(BOX) if (m + 1) // 2 % 2 == 0]
    odd = [m for m in range(BOX) if (m + 1) // 2 % 2 == 1]
    half = BOX // 2
    there = np.concatenate([basis[even, :half], basis[odd, :half]], 0)
    back = np.concatenate([basis[even, :half].T, basis[odd, :half].T], 0)
    halved = np.concatenate([green[:, even, :BOX], green[:, odd, :BOX]], 2)
    return green.reshape(-1, 2 * BOX), packed(halved, *four, left(there), left(back))


def split(value):
    high = value.astype(BF16)
    return high, (value - high.astype(F32)).astype(BF16)


def dot(a, b):
    return jnp.dot(a, b, preferred_element_type=F32)


def stacked(first, second):
    return jnp.concatenate([first, second], axis=1)


def target(pair_list, slot):
    size_x, size_y = lax.axis_size("dx"), lax.axis_size("dy")
    owner = pair_list[1, slot]
    rel_x = (owner // size_y - lax.axis_index("dx") + 1 + size_x) % size_x
    rel_y = (owner % size_y - lax.axis_index("dy") + 1 + size_y) % size_y
    return rel_x * 3 + rel_y


def known(i, j, offsets, pair_list, pair_mask):
    size_x, size_y = lax.axis_size("dx"), lax.axis_size("dy")
    here_x, here_y = lax.axis_index("dx"), lax.axis_index("dy")
    step = i * (1 - 2 * (here_x % 2))
    other = (here_x + step + size_x) % size_x * size_y + (here_y + j + size_y) % size_y
    mine = here_x * size_y + here_y
    move = tuple(offsets[c, mine] - offsets[c, other] for c in range(3))
    index = (1 + step) * 3 + 1 + j
    count = sum(jnp.where(target(pair_list, n) == index, pair_mask[n], 0) for n in range(pair_list.shape[1]))
    return move + (8 - index, count)


def unpack(tab, at, refs):
    lanes = 2 * BOX
    for ref in refs:
        size, width = ref.shape
        first = min(width, lanes)
        ref[:, pl.ds(0, first)] = tab[pl.ds(at, size), :][:, :first].astype(BF16)
        if width > lanes:
            ref[:, pl.ds(lanes, width - lanes)] = tab[pl.ds(at + size, size), :][:, : width - lanes].astype(BF16)
        at += 2 * size


def skewed(count, first, second):
    before = None
    for c in range(count):
        now = first(c)
        if before is not None:
            second(c - 1, before)
        before = now
    second(count - 1, before)


def three(value):
    high, rest = split(value)
    return jnp.concatenate([high, rest, high], 0)


def alone_kernel(own_ref, tab_hbm, green_hbm, out, own, green, wz, wzi, rf, ri, held, mid, mid2, tab, there, back, sems):
    tab_copy = pltpu.make_async_copy(tab_hbm, tab, sems.at[0])
    tab_copy.start()
    green_copy = pltpu.make_async_copy(green_hbm, green, sems.at[1])
    green_copy.start()
    lanes, half = 2 * BOX, BOX // 2
    low = lax.broadcasted_iota(jnp.int32, (BOX, lanes), 1) < BOX
    few = low[:half]
    sign = jnp.where(few, 1.0, -1.0)

    def turned(value):
        return pltpu.roll(value, BOX, 1)

    for t in range(half // 2):
        v = own_ref[:, pl.ds(t * lanes, lanes)].astype(F32)
        w = own_ref[:, pl.ds((t + half // 2) * lanes, lanes)].astype(F32)
        tv, tw = turned(v), turned(w)
        for y, value in ((2 * t, jnp.where(low, v, tv)), (2 * t + 1, jnp.where(low, tv, v))):
            own[pl.ds(y * BOX, BOX), :] = value
        for y, value in ((2 * t, jnp.where(low, w, tw)), (2 * t + 1, jnp.where(low, tw, w))):
            own[pl.ds((y + half) * BOX, BOX), :] = value
        held[pl.ds(2 * t * BOX, BOX), :] = jnp.where(low, v, tw)
        held[pl.ds((2 * t + 1) * BOX, BOX), :] = jnp.where(low, tv, w)

    tab_copy.wait()
    unpack(tab, GREEN // 2, (wz, wzi, rf, ri, there, back))

    def forward_first(c):
        rows = []
        for y in range(c * CHUNK, (c + 1) * CHUNK):
            v = held[pl.ds(y * BOX, BOX), :]
            rows.append(stacked(*split(v * v)))
        return dot(jnp.concatenate(rows, 0), wz[...])

    def forward_second(c, wave):
        wave = wave[:, :lanes] + wave[:, lanes:]
        for j in range(0, CHUNK, 2):
            y, at = c * CHUNK + j, j * BOX
            u = dot(rf[...], three(stacked(wave[at : at + BOX], wave[at + BOX : at + 2 * BOX])))
            mid[pl.ds(y, BOX, stride=HROW), :] = u[:, :lanes]
            mid[pl.ds(y + 1, BOX, stride=HROW), :] = u[:, lanes:]

    skewed(half // CHUNK, forward_first, forward_second)

    def crossed(value):
        return value * sign + turned(value)

    def chosen(value):
        return [jnp.where(few, value[:half, at : at + lanes], value[half:, at : at + lanes]) for at in (0, lanes)]

    def middle_first(c):
        waves = []
        for k in range(c * CHUNK, (c + 1) * CHUNK, 2):
            parts = [crossed(mid[pl.ds((k + q) * HROW, half), :]) for q in range(2)]
            waves.append(dot(there[...], three(stacked(*parts))))
        return waves

    def middle_second(c, waves):
        for j, wave in enumerate(waves):
            k = c * CHUNK + 2 * j
            parts = [v * tab[pl.ds((k + q + 1) // 2 * half, half), :] for q, v in enumerate(chosen(wave))]
            wave = dot(back[...], three(stacked(*parts)))
            for q, v in enumerate(chosen(wave)):
                mid2[pl.ds((k + q) * HROW, half), :] = crossed(v)

    skewed(BOX // CHUNK, middle_first, middle_second)

    tail = own_ref[pl.ds(0, 16), pl.ds(BOX * BOX, lanes)].astype(F32)[:8]
    at_lane = lax.broadcasted_iota(jnp.int32, (8, lanes), 1)
    weight = 2.0 * jnp.sum(jnp.where(at_lane == 4, tail, 0.0), axis=1, keepdims=True)[:1]

    def backward_first(c):
        waves = []
        for y in range(c * CHUNK, (c + 1) * CHUNK, 2):
            v = stacked(mid2[pl.ds(y, BOX, stride=HROW), :], mid2[pl.ds(y + 1, BOX, stride=HROW), :])
            waves.append(dot(ri[...], three(v)))
        return waves

    def backward_second(c, waves):
        rows = []
        for u in waves:
            high, rest = split(u)
            rows.append(stacked(high[:, :lanes], rest[:, :lanes]))
            rows.append(stacked(high[:, lanes:], rest[:, lanes:]))
        wave = dot(jnp.concatenate(rows, 0), wzi[...])
        field = wave[:, :lanes] + wave[:, lanes:]
        for j in range(0, CHUNK, 2):
            y = c * CHUNK + j
            v, w = [
                field[(j + q) * BOX : (j + q + 1) * BOX] * (held[pl.ds((y + q) * BOX, BOX), :] * weight)
                for q in range(2)
            ]
            out[:, pl.ds(y * BOX, lanes)] = jnp.where(low, v, turned(w))
            out[:, pl.ds((y + half) * BOX, lanes)] = jnp.where(low, turned(v), w)

    skewed(half // CHUNK, backward_first, backward_second)
    green_copy.wait()


def tail_kernel(list_hbm, mask_hbm, box_hbm, out, pair_list, pair_mask, sems):
    copies = [
        pltpu.make_async_copy(box_hbm, out.at[:, pl.ds(0, BOX * BOX)], sems.at[0]),
        pltpu.make_async_copy(list_hbm, pair_list, sems.at[1]),
        pltpu.make_async_copy(mask_hbm, pair_mask, sems.at[2]),
    ]
    for copy in copies:
        copy.start()
    copies[1].wait()
    copies[2].wait()
    lane = lax.broadcasted_iota(jnp.int32, (BOX, 2 * BOX), 1)
    counts = jnp.zeros((BOX, 2 * BOX), jnp.int32)
    for n in range(pair_list.shape[1]):
        counts += jnp.where(lane == target(pair_list, n), pair_mask[n], 0)
    out[:, pl.ds(BOX * BOX, 2 * BOX)] = counts.astype(F32).astype(BF16)
    copies[0].wait()


def kernel(places, last, offsets, pair_list, pair_mask, own_ref, *refs):
    pairs = len(places) // 2
    near, refs = refs[: 2 * pairs], refs[2 * pairs :]
    own = own_ref
    tab, wz, wzi, rf, ri, acc_in, out, *refs = refs
    if last:
        out_hbm, (out, out_sem, *refs) = out, refs
    held, mid, mid2 = refs
    facts = [known(i, j, offsets, pair_list, pair_mask) for i, j in places]
    lanes = 2 * BOX
    low = lax.broadcasted_iota(jnp.int32, (BOX, lanes), 1) < BOX

    row = lax.broadcasted_iota(jnp.int32, (4 * BOX, 4 * BOX), 0)
    col = lax.broadcasted_iota(jnp.int32, (4 * BOX, 4 * BOX), 1)
    row_half, col_half = row // lanes, (col // BOX) % 2
    same = (row_half == col_half) & ((row // BOX) % 2 == col // lanes)
    away = row % BOX - col % BOX

    for y in range(BOX + 1):
        held[pl.ds(y * ROW, ROW - BOX), :] = jnp.zeros((ROW - BOX, lanes), F32)
    held[pl.ds(BOX * ROW, ROW + 32), :] = jnp.zeros((ROW + 32, lanes), F32)

    def out_copy(c):
        at = pl.ds(c * CHUNK * BOX, CHUNK * BOX)
        return pltpu.make_async_copy(out.at[:, at], out_hbm.at[:, at], out_sem.at[c])

    for p in range(pairs):
        a_ref, b_ref = near[2 * p], near[2 * p + 1]
        sx, sy, sz, slot, count = zip(*facts[2 * p : 2 * p + 2])

        def weight(ref, h):
            tail = ref[pl.ds(0, 16), pl.ds(BOX * BOX, lanes)].astype(F32)[:8]
            at = lax.broadcasted_iota(jnp.int32, (8, lanes), 1)
            sent = jnp.sum(jnp.where(at == slot[h], tail, 0.0), axis=1, keepdims=True)[:1]
            return sent + count[h].astype(F32)

        def solve():
            want = jnp.where(col_half == 0, sz[0], sz[1])
            pick = jnp.where(same & (away == want), 1.0, 0.0).astype(BF16)

            def load():
                for t0 in range(0, BOX // 2, THICK):
                    rows = []
                    for t in range(t0, t0 + THICK):
                        at = pl.ds(t * lanes, lanes)
                        rows.append(stacked(a_ref[:, at], b_ref[:, at]))
                    v = dot(jnp.concatenate(rows, 0), pick)
                    for t in range(t0, t0 + THICK):
                        base = t * (2 * ROW) + (ROW - BOX)
                        part = v[(t - t0) * BOX : (t - t0 + 1) * BOX]
                        held[pl.ds(base, BOX), :] = part[:, :lanes]
                        held[pl.ds(base + ROW, BOX), :] = part[:, lanes:]

            def partner(y):
                parts = []
                for h in range(2):
                    from_y = y + sy[h]
                    block = jnp.where((from_y >= 0) & (from_y < BOX), from_y, BOX)
                    parts.append(held[pl.ds(block * ROW + (ROW - BOX) + sx[h], BOX), :])
                return jnp.where(low, parts[0], parts[1])

            def forward():
                def first(c):
                    rows = []
                    for j in range(CHUNK):
                        y = c * CHUNK + j
                        rows.append(stacked(*split(partner(y) * own[pl.ds(y * BOX, BOX), :])))
                    return dot(jnp.concatenate(rows, 0), wz[...])

                def second(c, wave):
                    high, rest = split(wave[:, :lanes] + wave[:, lanes:])
                    for j in range(0, CHUNK, 2):
                        at = j * BOX
                        h = stacked(high[at : at + BOX], high[at + BOX : at + 2 * BOX])
                        l = stacked(rest[at : at + BOX], rest[at + BOX : at + 2 * BOX])
                        u = dot(rf[...], jnp.concatenate([h, l, h], 0))
                        y = c * CHUNK + j
                        mid[pl.ds(y, BOX, stride=MROW), :] = u[:, :lanes]
                        mid[pl.ds(y + 1, BOX, stride=MROW), :] = u[:, lanes:]

                skewed(BOX // CHUNK, first, second)

            def green(k):
                return tab[pl.ds(k * BOX, BOX), :]

            def middle():
                def first(c):
                    waves = []
                    for j in range(0, CHUNK, 2):
                        base = (c * CHUNK + j) * MROW
                        h, l = split(stacked(mid[pl.ds(base, BOX), :], mid[pl.ds(base + MROW, BOX), :]))
                        waves.append(dot(rf[...], jnp.concatenate([h, l, h], 0)))
                    return waves

                def second(c, waves):
                    for j in range(0, CHUNK, 2):
                        k = c * CHUNK + j
                        base = k * MROW
                        h, l = split(waves[j // 2] * stacked(green((k + 1) // 2), green((k + 2) // 2)))
                        v = dot(ri[...], jnp.concatenate([h, l, h], 0))
                        mid2[pl.ds(base, BOX), :] = v[:, :lanes]
                        mid2[pl.ds(base + MROW, BOX), :] = v[:, lanes:]

                skewed(BOX // CHUNK, first, second)

            def backward():
                scale = jnp.where(low, weight(a_ref, 0), weight(b_ref, 1))

                def first(c):
                    waves = []
                    for j in range(0, CHUNK, 2):
                        y = c * CHUNK + j
                        v = stacked(mid2[pl.ds(y, BOX, stride=MROW), :], mid2[pl.ds(y + 1, BOX, stride=MROW), :])
                        h, l = split(v)
                        waves.append(dot(ri[...], jnp.concatenate([h, l, h], 0)))
                    return waves

                def second(c, waves):
                    rows = []
                    for u in waves:
                        h, l = split(u)
                        rows.append(stacked(h[:, :lanes], l[:, :lanes]))
                        rows.append(stacked(h[:, lanes:], l[:, lanes:]))
                    wave = dot(jnp.concatenate(rows, 0), wzi[...])
                    field = wave[:, :lanes] + wave[:, lanes:]
                    for j in range(0, CHUNK, 2):
                        y = c * CHUNK + j
                        parts = []
                        for k in range(2):
                            v = field[(j + k) * BOX : (j + k + 1) * BOX] * (partner(y + k) * scale)
                            parts.append(v + pltpu.roll(v, BOX, 1))
                        at = pl.ds(y * BOX, lanes)
                        both = jnp.where(low, parts[0], parts[1])
                        if p > 0:
                            both = out[:, at] + both
                        else:
                            both = acc_in[:, at] + both
                        out[:, at] = both
                    if last and p == pairs - 1:
                        out_copy(c).start()

                skewed(BOX // CHUNK, first, second)

            load()
            forward()
            middle()
            backward()

        solve()

    if last:
        for c in range(BOX // CHUNK):
            out_copy(c).wait()


SMEM = pl.BlockSpec(memory_space=pltpu.SMEM)
HBM = pl.BlockSpec(memory_space=pltpu.HBM)
VMEM = pl.BlockSpec(memory_space=pltpu.VMEM)
PARAMS = pltpu.CompilerParams(vmem_limit_bytes=28 * 1024 * 1024)


def in_hbm(value):
    return pltpu.with_memory_space_constraint(jnp.asarray(value), pltpu.HBM)


def own_term(own):
    lanes = 2 * BOX
    green, table = tables()
    rows = pltpu.VMEM((BOX * HROW, lanes), F32)
    shapes = [((BOX, BOX * BOX), F32), ((BOX * BOX, lanes), F32), (green.shape, F32)]
    shapes += [((2 * lanes, 2 * lanes), BF16)] * 2 + [((BOX, 3 * BOX), BF16)] * 2
    acc, *shared = pl.pallas_call(
        alone_kernel,
        out_shape=[jax.ShapeDtypeStruct(*shape) for shape in shapes],
        in_specs=[VMEM, HBM, HBM],
        out_specs=[VMEM] * len(shapes),
        scratch_shapes=[pltpu.VMEM((BOX * BOX // 2, lanes), F32), rows, rows, pltpu.VMEM(table.shape, F32)]
        + [pltpu.VMEM((BOX, 3 * BOX // 2), BF16)] * 2
        + [pltpu.SemaphoreType.DMA((2,))],
        compiler_params=PARAMS,
    )(own, in_hbm(table), in_hbm(green))
    return acc, shared


def exchange_terms(places, ints, shared, boxes, acc, last=False):
    lanes = 2 * BOX
    sink = [pltpu.VMEM((BOX, BOX * BOX), F32), pltpu.SemaphoreType.DMA((BOX // CHUNK,))] if last else []
    rows = pltpu.VMEM((BOX * MROW, lanes), F32)
    own, *tabs = shared
    return pl.pallas_call(
        functools.partial(kernel, places, last),
        out_shape=jax.ShapeDtypeStruct((BOX, BOX * BOX), F32),
        in_specs=[SMEM] * 3 + [VMEM] * (2 + len(boxes) + len(tabs)),
        out_specs=HBM if last else VMEM,
        scratch_shapes=sink + [pltpu.VMEM(((BOX + 1) * ROW + 32, lanes), F32), rows, rows],
        compiler_params=PARAMS,
    )(*ints, own, *boxes, *tabs, acc)


def along(value, axis, to):
    return lax.ppermute(value, axis, [(i, to(i)) for i in range(lax.axis_size(axis))])


def body(orbitals, offsets, pair_list, pair_mask):
    size_x, size_y = lax.axis_size("dx"), lax.axis_size("dy")
    ints = (offsets.T, pair_list.T, pair_mask)
    own = pl.pallas_call(
        tail_kernel,
        out_shape=jax.ShapeDtypeStruct((BOX, BOX * BOX + 2 * BOX), BF16),
        in_specs=[HBM] * 3,
        out_specs=VMEM,
        scratch_shapes=[
            pltpu.SMEM(ints[1].shape, jnp.int32),
            pltpu.SMEM(pair_mask.shape, jnp.int32),
            pltpu.SemaphoreType.DMA((3,)),
        ],
        compiler_params=PARAMS,
    )(in_hbm(ints[1]), in_hbm(pair_mask), in_hbm(orbitals[0]))

    def inner(i):
        return i ^ 1

    def outer(i):
        return (i - 1 + 2 * (i % 2)) % size_x

    x_far, x_near = along(own, "dx", outer), along(own, "dx", inner)
    y_last = along(own, "dy", lambda i: (i + 1) % size_y)
    y_next = along(own, "dy", lambda i: (i - 1) % size_y)
    acc, shared = own_term(own)
    acc = exchange_terms(((1, 0), (-1, 0)), ints, shared, (x_near, x_far), acc)
    y_next, y_last, acc = lax.optimization_barrier((y_next, y_last, acc))
    corners = [along(v, "dx", to) for to in (inner, outer) for v in (y_next, y_last)]
    acc = exchange_terms(((0, 1), (0, -1)), ints, shared, (y_next, y_last), acc)
    acc = exchange_terms(((1, 1), (1, -1)), ints, shared, corners[:2], acc)
    acc = exchange_terms(((-1, 1), (-1, -1)), ints, shared, corners[2:], acc, last=True)
    return acc[None]


def solution(mesh):
    placed = (P(("dx", "dy"), None, None), P(), P(("dx", "dy"), None), P(("dx", "dy")))
    return jax.shard_map(
        body, mesh=mesh, in_specs=placed, out_specs=P(("dx", "dy"), None, None), check_vma=False
    )
```

```python
import functools
import math

import jax
import jax.numpy as jnp
import numpy as np
import ml_dtypes
from jax import lax
from jax.experimental import pallas as pl
from jax.experimental.pallas import tpu as pltpu
from jax.sharding import PartitionSpec as P

BOX = 64
ROW = 96
GREEN = (BOX // 2 + 1) * BOX
MROW = 72
HROW = 40
CHUNK = 16
WIDE = 32
SMALL = 8
THICK = 8
F32 = jnp.float32
BF16 = jnp.bfloat16


def tables():
    n = np.arange(BOX)
    basis = np.zeros((BOX, BOX))
    basis[0] = 1.0
    for m in range(1, BOX // 2):
        basis[2 * m - 1] = math.sqrt(2.0) * np.cos(2.0 * np.pi * m * n / BOX)
        basis[2 * m] = math.sqrt(2.0) * np.sin(2.0 * np.pi * m * n / BOX)
    basis[BOX - 1] = (-1.0) ** n
    basis /= math.sqrt(BOX)

    def cut(value):
        high = value.astype(ml_dtypes.bfloat16)
        low = (value - high.astype(np.float64)).astype(ml_dtypes.bfloat16)
        return high, low

    def right(matrix):
        both = np.kron(np.eye(2), matrix)
        high, low = cut(both)
        half = np.concatenate([high, low], 1)
        return np.concatenate([half, half], 0)

    def left(matrix):
        high, low = cut(matrix)
        return np.concatenate([high, high, low], 1)

    square = (2.0 * np.pi / BOX * ((n + 1) // 2)) ** 2
    some = (2.0 * np.pi / BOX * np.arange(BOX // 2 + 1)) ** 2
    total = some[:, None, None] + square[None, :, None] + np.concatenate([square, square])[None, None, :]
    green = (1.0 / (total + (8.0 * np.pi / BOX) ** 2)).astype(np.float32)
    def packed(first, *tables):
        blocks = [first.reshape(-1, 2 * BOX)]
        for wide in tables:
            wide = np.pad(wide.astype(np.float32), ((0, 0), (0, 4 * BOX - wide.shape[1])))
            blocks += [wide[:, : 2 * BOX], wide[:, 2 * BOX :]]
        return np.concatenate(blocks, 0)

    four = (right(basis.T), right(basis), left(basis), left(basis.T))
    even = [m for m in range(BOX) if (m + 1) // 2 % 2 == 0]
    odd = [m for m in range(BOX) if (m + 1) // 2 % 2 == 1]
    half = BOX // 2
    there = np.concatenate([basis[even, :half], basis[odd, :half]], 0)
    back = np.concatenate([basis[even, :half].T, basis[odd, :half].T], 0)
    halved = np.concatenate([green[:, even, :BOX], green[:, odd, :BOX]], 2)
    return green.reshape(-1, 2 * BOX), packed(halved, *four, left(there), left(back))


def split(value):
    high = value.astype(BF16)
    return high, (value - high.astype(F32)).astype(BF16)


def dot(a, b):
    return jnp.dot(a, b, preferred_element_type=F32)


def stacked(first, second):
    return jnp.concatenate([first, second], axis=1)


def target(pair_list, slot):
    size_x, size_y = lax.axis_size("dx"), lax.axis_size("dy")
    owner = pair_list[1, slot]
    rel_x = (owner // size_y - lax.axis_index("dx") + 1 + size_x) % size_x
    rel_y = (owner % size_y - lax.axis_index("dy") + 1 + size_y) % size_y
    return rel_x * 3 + rel_y


def known(i, j, offsets, pair_list, pair_mask):
    size_x, size_y = lax.axis_size("dx"), lax.axis_size("dy")
    here_x, here_y = lax.axis_index("dx"), lax.axis_index("dy")
    step = i * (1 - 2 * (here_x % 2))
    other = (here_x + step + size_x) % size_x * size_y + (here_y + j + size_y) % size_y
    mine = here_x * size_y + here_y
    move = tuple(offsets[c, mine] - offsets[c, other] for c in range(3))
    index = (1 + step) * 3 + 1 + j
    count = sum(jnp.where(target(pair_list, n) == index, pair_mask[n], 0) for n in range(pair_list.shape[1]))
    return move + (8 - index, count)


def unpack(tab, at, refs):
    lanes = 2 * BOX
    for ref in refs:
        size, width = ref.shape
        first = min(width, lanes)
        ref[:, pl.ds(0, first)] = tab[pl.ds(at, size), :][:, :first].astype(BF16)
        if width > lanes:
            ref[:, pl.ds(lanes, width - lanes)] = tab[pl.ds(at + size, size), :][:, : width - lanes].astype(BF16)
        at += 2 * size


def skewed(count, first, second):
    before = None
    for c in range(count):
        now = first(c)
        if before is not None:
            second(c - 1, before)
        before = now
    second(count - 1, before)


def three(value):
    high, rest = split(value)
    return jnp.concatenate([high, rest, high], 0)


def alone_kernel(own_ref, tab_hbm, green_hbm, out, own, green, wz, wzi, rf, ri, held, mid, mid2, tab, there, back, sems):
    tab_copy = pltpu.make_async_copy(tab_hbm, tab, sems.at[0])
    tab_copy.start()
    green_copy = pltpu.make_async_copy(green_hbm, green, sems.at[1])
    green_copy.start()
    lanes, half = 2 * BOX, BOX // 2
    low = lax.broadcasted_iota(jnp.int32, (BOX, lanes), 1) < BOX
    few = low[:half]
    sign = jnp.where(few, 1.0, -1.0)

    def turned(value):
        return pltpu.roll(value, BOX, 1)

    for t in range(half // 2):
        v = own_ref[:, pl.ds(t * lanes, lanes)].astype(F32)
        w = own_ref[:, pl.ds((t + half // 2) * lanes, lanes)].astype(F32)
        tv, tw = turned(v), turned(w)
        for y, value in ((2 * t, jnp.where(low, v, tv)), (2 * t + 1, jnp.where(low, tv, v))):
            own[pl.ds(y * BOX, BOX), :] = value
        for y, value in ((2 * t, jnp.where(low, w, tw)), (2 * t + 1, jnp.where(low, tw, w))):
            own[pl.ds((y + half) * BOX, BOX), :] = value
        held[pl.ds(2 * t * BOX, BOX), :] = jnp.where(low, v, tw)
        held[pl.ds((2 * t + 1) * BOX, BOX), :] = jnp.where(low, tv, w)

    tab_copy.wait()
    unpack(tab, GREEN // 2, (wz, wzi, rf, ri, there, back))

    def forward_first(c):
        rows = []
        for y in range(c * CHUNK, (c + 1) * CHUNK):
            v = held[pl.ds(y * BOX, BOX), :]
            rows.append(stacked(*split(v * v)))
        return dot(jnp.concatenate(rows, 0), wz[...])

    def forward_second(c, wave):
        wave = wave[:, :lanes] + wave[:, lanes:]
        for j in range(0, CHUNK, 2):
            y, at = c * CHUNK + j, j * BOX
            u = dot(rf[...], three(stacked(wave[at : at + BOX], wave[at + BOX : at + 2 * BOX])))
            mid[pl.ds(y, BOX, stride=HROW), :] = u[:, :lanes]
            mid[pl.ds(y + 1, BOX, stride=HROW), :] = u[:, lanes:]

    skewed(half // CHUNK, forward_first, forward_second)

    def crossed(value):
        return value * sign + turned(value)

    def chosen(value):
        return [jnp.where(few, value[:half, at : at + lanes], value[half:, at : at + lanes]) for at in (0, lanes)]

    def middle_first(c):
        waves = []
        for k in range(c * CHUNK, (c + 1) * CHUNK, 2):
            parts = [crossed(mid[pl.ds((k + q) * HROW, half), :]) for q in range(2)]
            waves.append(dot(there[...], three(stacked(*parts))))
        return waves

    def middle_second(c, waves):
        for j, wave in enumerate(waves):
            k = c * CHUNK + 2 * j
            parts = [v * tab[pl.ds((k + q + 1) // 2 * half, half), :] for q, v in enumerate(chosen(wave))]
            wave = dot(back[...], three(stacked(*parts)))
            for q, v in enumerate(chosen(wave)):
                mid2[pl.ds((k + q) * HROW, half), :] = crossed(v)

    skewed(BOX // CHUNK, middle_first, middle_second)

    tail = own_ref[pl.ds(0, 16), pl.ds(BOX * BOX, lanes)].astype(F32)[:8]
    at_lane = lax.broadcasted_iota(jnp.int32, (8, lanes), 1)
    weight = 2.0 * jnp.sum(jnp.where(at_lane == 4, tail, 0.0), axis=1, keepdims=True)[:1]

    def backward_first(c):
        waves = []
        for y in range(c * CHUNK, (c + 1) * CHUNK, 2):
            v = stacked(mid2[pl.ds(y, BOX, stride=HROW), :], mid2[pl.ds(y + 1, BOX, stride=HROW), :])
            waves.append(dot(ri[...], three(v)))
        return waves

    def backward_second(c, waves):
        rows = []
        for u in waves:
            high, rest = split(u)
            rows.append(stacked(high[:, :lanes], rest[:, :lanes]))
            rows.append(stacked(high[:, lanes:], rest[:, lanes:]))
        wave = dot(jnp.concatenate(rows, 0), wzi[...])
        field = wave[:, :lanes] + wave[:, lanes:]
        for j in range(0, CHUNK, 2):
            y = c * CHUNK + j
            v, w = [
                field[(j + q) * BOX : (j + q + 1) * BOX] * (held[pl.ds((y + q) * BOX, BOX), :] * weight)
                for q in range(2)
            ]
            out[:, pl.ds(y * BOX, lanes)] = jnp.where(low, v, turned(w))
            out[:, pl.ds((y + half) * BOX, lanes)] = jnp.where(low, turned(v), w)

    skewed(half // CHUNK, backward_first, backward_second)
    green_copy.wait()


def tail_kernel(list_hbm, mask_hbm, box_hbm, out, pair_list, pair_mask, sems):
    copies = [
        pltpu.make_async_copy(box_hbm, out.at[:, pl.ds(0, BOX * BOX)], sems.at[0]),
        pltpu.make_async_copy(list_hbm, pair_list, sems.at[1]),
        pltpu.make_async_copy(mask_hbm, pair_mask, sems.at[2]),
    ]
    for copy in copies:
        copy.start()
    copies[1].wait()
    copies[2].wait()
    lane = lax.broadcasted_iota(jnp.int32, (BOX, 2 * BOX), 1)
    counts = jnp.zeros((BOX, 2 * BOX), jnp.int32)
    for n in range(pair_list.shape[1]):
        counts += jnp.where(lane == target(pair_list, n), pair_mask[n], 0)
    out[:, pl.ds(BOX * BOX, 2 * BOX)] = counts.astype(F32).astype(BF16)
    copies[0].wait()


def kernel(places, last, offsets, pair_list, pair_mask, own_ref, *refs):
    pairs = len(places) // 2
    near, refs = refs[: 2 * pairs], refs[2 * pairs :]
    own = own_ref
    tab, wz, wzi, rf, ri, acc_in, out, *refs = refs
    if last:
        out_hbm, (out, out_sem, *refs) = out, refs
    held, mid, mid2 = refs
    facts = [known(i, j, offsets, pair_list, pair_mask) for i, j in places]
    lanes = 2 * BOX
    low = lax.broadcasted_iota(jnp.int32, (BOX, lanes), 1) < BOX

    row = lax.broadcasted_iota(jnp.int32, (4 * BOX, 4 * BOX), 0)
    col = lax.broadcasted_iota(jnp.int32, (4 * BOX, 4 * BOX), 1)
    row_half, col_half = row // lanes, (col // BOX) % 2
    same = (row_half == col_half) & ((row // BOX) % 2 == col // lanes)
    away = row % BOX - col % BOX

    for y in range(BOX + 1):
        held[pl.ds(y * ROW, ROW - BOX), :] = jnp.zeros((ROW - BOX, lanes), F32)
    held[pl.ds(BOX * ROW, ROW + 32), :] = jnp.zeros((ROW + 32, lanes), F32)

    def out_copy(c):
        at = pl.ds(c * CHUNK * BOX, CHUNK * BOX)
        return pltpu.make_async_copy(out.at[:, at], out_hbm.at[:, at], out_sem.at[c])

    for p in range(pairs):
        a_ref, b_ref = near[2 * p], near[2 * p + 1]
        sx, sy, sz, slot, count = zip(*facts[2 * p : 2 * p + 2])

        def weight(ref, h):
            tail = ref[pl.ds(0, 16), pl.ds(BOX * BOX, lanes)].astype(F32)[:8]
            at = lax.broadcasted_iota(jnp.int32, (8, lanes), 1)
            sent = jnp.sum(jnp.where(at == slot[h], tail, 0.0), axis=1, keepdims=True)[:1]
            return sent + count[h].astype(F32)

        def solve():
            want = jnp.where(col_half == 0, sz[0], sz[1])
            pick = jnp.where(same & (away == want), 1.0, 0.0).astype(BF16)

            def load():
                for t0 in range(0, BOX // 2, THICK):
                    rows = []
                    for t in range(t0, t0 + THICK):
                        at = pl.ds(t * lanes, lanes)
                        rows.append(stacked(a_ref[:, at], b_ref[:, at]))
                    v = dot(jnp.concatenate(rows, 0), pick)
                    for t in range(t0, t0 + THICK):
                        base = t * (2 * ROW) + (ROW - BOX)
                        part = v[(t - t0) * BOX : (t - t0 + 1) * BOX]
                        held[pl.ds(base, BOX), :] = part[:, :lanes]
                        held[pl.ds(base + ROW, BOX), :] = part[:, lanes:]

            def partner(y):
                parts = []
                for h in range(2):
                    from_y = y + sy[h]
                    block = jnp.where((from_y >= 0) & (from_y < BOX), from_y, BOX)
                    parts.append(held[pl.ds(block * ROW + (ROW - BOX) + sx[h], BOX), :])
                return jnp.where(low, parts[0], parts[1])

            def forward():
                def first(c):
                    rows = []
                    for j in range(WIDE):
                        y = c * WIDE + j
                        rows.append(stacked(*split(partner(y) * own[pl.ds(y * BOX, BOX), :])))
                    return dot(jnp.concatenate(rows, 0), wz[...])

                def second(c, wave):
                    high, rest = split(wave[:, :lanes] + wave[:, lanes:])
                    for j in range(0, WIDE, 2):
                        at = j * BOX
                        h = stacked(high[at : at + BOX], high[at + BOX : at + 2 * BOX])
                        l = stacked(rest[at : at + BOX], rest[at + BOX : at + 2 * BOX])
                        u = dot(rf[...], jnp.concatenate([h, l, h], 0))
                        y = c * WIDE + j
                        mid[pl.ds(y, BOX, stride=MROW), :] = u[:, :lanes]
                        mid[pl.ds(y + 1, BOX, stride=MROW), :] = u[:, lanes:]

                skewed(BOX // WIDE, first, second)

            def green(k):
                return tab[pl.ds(k * BOX, BOX), :]

            def middle():
                def first(c):
                    waves = []
                    for j in range(0, SMALL, 2):
                        base = (c * SMALL + j) * MROW
                        h, l = split(stacked(mid[pl.ds(base, BOX), :], mid[pl.ds(base + MROW, BOX), :]))
                        waves.append(dot(rf[...], jnp.concatenate([h, l, h], 0)))
                    return waves

                def second(c, waves):
                    for j in range(0, SMALL, 2):
                        k = c * SMALL + j
                        base = k * MROW
                        h, l = split(waves[j // 2] * stacked(green((k + 1) // 2), green((k + 2) // 2)))
                        v = dot(ri[...], jnp.concatenate([h, l, h], 0))
                        mid2[pl.ds(base, BOX), :] = v[:, :lanes]
                        mid2[pl.ds(base + MROW, BOX), :] = v[:, lanes:]

                skewed(BOX // SMALL, first, second)

            def backward():
                scale = jnp.where(low, weight(a_ref, 0), weight(b_ref, 1))

                def first(c):
                    waves = []
                    for j in range(0, CHUNK, 2):
                        y = c * CHUNK + j
                        v = stacked(mid2[pl.ds(y, BOX, stride=MROW), :], mid2[pl.ds(y + 1, BOX, stride=MROW), :])
                        h, l = split(v)
                        waves.append(dot(ri[...], jnp.concatenate([h, l, h], 0)))
                    return waves

                def second(c, waves):
                    rows = []
                    for u in waves:
                        h, l = split(u)
                        rows.append(stacked(h[:, :lanes], l[:, :lanes]))
                        rows.append(stacked(h[:, lanes:], l[:, lanes:]))
                    wave = dot(jnp.concatenate(rows, 0), wzi[...])
                    field = wave[:, :lanes] + wave[:, lanes:]
                    for j in range(0, CHUNK, 2):
                        y = c * CHUNK + j
                        parts = []
                        for k in range(2):
                            v = field[(j + k) * BOX : (j + k + 1) * BOX] * (partner(y + k) * scale)
                            parts.append(v + pltpu.roll(v, BOX, 1))
                        at = pl.ds(y * BOX, lanes)
                        both = jnp.where(low, parts[0], parts[1])
                        if p > 0:
                            both = out[:, at] + both
                        else:
                            both = acc_in[:, at] + both
                        out[:, at] = both
                    if last and p == pairs - 1:
                        out_copy(c).start()

                skewed(BOX // CHUNK, first, second)

            load()
            forward()
            middle()
            backward()

        solve()

    if last:
        for c in range(BOX // CHUNK):
            out_copy(c).wait()


SMEM = pl.BlockSpec(memory_space=pltpu.SMEM)
HBM = pl.BlockSpec(memory_space=pltpu.HBM)
VMEM = pl.BlockSpec(memory_space=pltpu.VMEM)
PARAMS = pltpu.CompilerParams(vmem_limit_bytes=28 * 1024 * 1024)


def in_hbm(value):
    return pltpu.with_memory_space_constraint(jnp.asarray(value), pltpu.HBM)


def own_term(own):
    lanes = 2 * BOX
    green, table = tables()
    rows = pltpu.VMEM((BOX * HROW, lanes), F32)
    shapes = [((BOX, BOX * BOX), F32), ((BOX * BOX, lanes), F32), (green.shape, F32)]
    shapes += [((2 * lanes, 2 * lanes), BF16)] * 2 + [((BOX, 3 * BOX), BF16)] * 2
    acc, *shared = pl.pallas_call(
        alone_kernel,
        out_shape=[jax.ShapeDtypeStruct(*shape) for shape in shapes],
        in_specs=[VMEM, HBM, HBM],
        out_specs=[VMEM] * len(shapes),
        scratch_shapes=[pltpu.VMEM((BOX * BOX // 2, lanes), F32), rows, rows, pltpu.VMEM(table.shape, F32)]
        + [pltpu.VMEM((BOX, 3 * BOX // 2), BF16)] * 2
        + [pltpu.SemaphoreType.DMA((2,))],
        compiler_params=PARAMS,
    )(own, in_hbm(table), in_hbm(green))
    return acc, shared


def exchange_terms(places, ints, shared, boxes, acc, last=False):
    lanes = 2 * BOX
    sink = [pltpu.VMEM((BOX, BOX * BOX), F32), pltpu.SemaphoreType.DMA((BOX // CHUNK,))] if last else []
    rows = pltpu.VMEM((BOX * MROW, lanes), F32)
    own, *tabs = shared
    return pl.pallas_call(
        functools.partial(kernel, places, last),
        out_shape=jax.ShapeDtypeStruct((BOX, BOX * BOX), F32),
        in_specs=[SMEM] * 3 + [VMEM] * (2 + len(boxes) + len(tabs)),
        out_specs=HBM if last else VMEM,
        scratch_shapes=sink + [pltpu.VMEM(((BOX + 1) * ROW + 32, lanes), F32), rows, rows],
        compiler_params=PARAMS,
    )(*ints, own, *boxes, *tabs, acc)


def along(value, axis, to):
    return lax.ppermute(value, axis, [(i, to(i)) for i in range(lax.axis_size(axis))])


def body(orbitals, offsets, pair_list, pair_mask):
    size_x, size_y = lax.axis_size("dx"), lax.axis_size("dy")
    ints = (offsets.T, pair_list.T, pair_mask)
    own = pl.pallas_call(
        tail_kernel,
        out_shape=jax.ShapeDtypeStruct((BOX, BOX * BOX + 2 * BOX), BF16),
        in_specs=[HBM] * 3,
        out_specs=VMEM,
        scratch_shapes=[
            pltpu.SMEM(ints[1].shape, jnp.int32),
            pltpu.SMEM(pair_mask.shape, jnp.int32),
            pltpu.SemaphoreType.DMA((3,)),
        ],
        compiler_params=PARAMS,
    )(in_hbm(ints[1]), in_hbm(pair_mask), in_hbm(orbitals[0]))

    def inner(i):
        return i ^ 1

    def outer(i):
        return (i - 1 + 2 * (i % 2)) % size_x

    x_far, x_near = along(own, "dx", outer), along(own, "dx", inner)
    y_last = along(own, "dy", lambda i: (i + 1) % size_y)
    y_next = along(own, "dy", lambda i: (i - 1) % size_y)
    acc, shared = own_term(own)
    acc = exchange_terms(((1, 0), (-1, 0)), ints, shared, (x_near, x_far), acc)
    y_next, y_last, acc = lax.optimization_barrier((y_next, y_last, acc))
    corners = [along(v, "dx", to) for to in (inner, outer) for v in (y_next, y_last)]
    acc = exchange_terms(((0, 1), (0, -1)), ints, shared, (y_next, y_last), acc)
    acc = exchange_terms(((1, 1), (1, -1)), ints, shared, corners[:2], acc)
    acc = exchange_terms(((-1, 1), (-1, -1)), ints, shared, corners[2:], acc, last=True)
    return acc[None]


def solution(mesh):
    placed = (P(("dx", "dy"), None, None), P(), P(("dx", "dy"), None), P(("dx", "dy")))
    return jax.shard_map(
        body, mesh=mesh, in_specs=placed, out_specs=P(("dx", "dy"), None, None), check_vma=False
    )
```
